256 devices in a mesh: dx: 16 (over x, z_lo), dy: 16 (over z_hi, y, core).
Axes of the slice: x: 4, y: 4, z: 8 (z_hi: 2, z_lo: 4; z = z_hi * 4 + z_lo), core: 2. Of those that a mesh axis runs over, the one named last changes fastest.
Arguments:
- queries: bfloat16 [98304, 1024], P(('dx', 'dy')), may hold values from -1.25 to 1.25
- documents: bfloat16 [98304, 1024], P(('dx', 'dy')), may hold values from -8 to 10
- positives: int32 [98304], P(('dx', 'dy')), may hold values from 0 to 98303, as said below
Outputs:
- row_loss: float32 [98304], P(('dx', 'dy'))
- grad_queries: float32 [98304, 1024], P(('dx', 'dy'))
- grad_documents: float32 [98304, 1024], P(('dx', 'dy'))
The draws below stay inside these ranges and needn't reach their ends.
Inputs may be any that keep to these rules, and one draw needn't show every extreme that they name: positives[i] lies in the block of 384 rows that holds row i, and within each block every row is the positive of exactly one query.
All inputs are finite; a program needn't handle non-finite values.
Results may differ from the reference program's by a relative error of at most 0.0028.
Values may be sent and summed in bfloat16 or wider, within the bound.
A program may use at most 64 MiB of HBM per device.

```python
import math
import jax
import jax.numpy as jnp
from jax import lax

E = 1024
ROWS_DEV = 384
BATCH = 98304
STRIDE = 17
ROUNDS = 4


def pick_rows(row_key):
    return jax.random.permutation(row_key, ROWS_DEV)[:6]


def shuffle_rows(block_key):
    return jax.random.permutation(block_key, ROWS_DEV)


def layout(key):
    blocks = BATCH // ROWS_DEV
    row_keys = jax.random.split(jax.random.fold_in(key, 11), blocks)
    chosen_rows = jax.vmap(pick_rows)(row_keys)
    chosen_cols = jax.random.permutation(jax.random.fold_in(key, 12), E)[:3]
    return (chosen_rows, chosen_cols)


def plant(bulk, chosen_rows, chosen_cols, leading, trailing):
    bulk = jnp.clip(bulk, -1.0, 1.0)
    position = jnp.arange(ROWS_DEV)
    column = jnp.arange(E)
    reserved = jnp.any(column[:, None] == chosen_cols[None, :], axis=1)
    bulk = jnp.where(reserved[None, None, :], 0.0, bulk)
    result = bulk
    for group in range(3):
        col_hit = column == chosen_cols[group]
        for member, levels in ((0, leading), (1, trailing)):
            row_hit = position[None, :] == chosen_rows[:, 2 * group + member][:, None]
            planted = jnp.where(col_hit[None, None, :], levels[group], 0.05 * bulk)
            result = jnp.where(row_hit[:, :, None], planted, result)
    return result.reshape(BATCH, E)


def draw_queries(key, part):
    chosen_rows, chosen_cols = layout(key)
    key = jax.random.fold_in(key, 3)
    scale_key, bulk_key = jax.random.split(key)
    full_shape = (BATCH // ROWS_DEV, ROWS_DEV, E)
    amplitude = 0.447 * float(E) ** (-0.25)
    scales = jnp.exp(jax.random.uniform(scale_key, full_shape[:2] + (1,), jnp.float32, math.log(0.6), math.log(1.6)))
    bulk = jax.random.normal(bulk_key, full_shape, jnp.float32) * amplitude * scales
    leading = (1.25, -1.25, 1.25)
    trailing = (1.25 - 0.1 / 6.0, -(1.25 - 0.1 / 8.0), 1.25 - 0.1 / 10.0)
    return plant(bulk, chosen_rows, chosen_cols, leading, trailing).astype(jnp.bfloat16)


def draw_documents(key, part):
    chosen_rows, chosen_cols = layout(key)
    key = jax.random.fold_in(key, 5)
    scale_key, bulk_key = jax.random.split(key)
    full_shape = (BATCH // ROWS_DEV, ROWS_DEV, E)
    amplitude = 0.447 * float(E) ** (-0.25)
    scales = jnp.exp(jax.random.uniform(scale_key, full_shape[:2] + (1,), jnp.float32, math.log(0.6), math.log(1.6)))
    bulk = jax.random.normal(bulk_key, full_shape, jnp.float32) * amplitude * scales
    leading = (6.0, -8.0, 10.0)
    trailing = (5.92, -7.92, 9.92)
    return plant(bulk, chosen_rows, chosen_cols, leading, trailing).astype(jnp.bfloat16)


def draw_positives(key, part):
    key = jax.random.fold_in(key, 7)
    blocks = BATCH // ROWS_DEV
    block_keys = jax.random.split(key, blocks)
    orders = jax.vmap(shuffle_rows)(block_keys)
    starts = jnp.arange(blocks, dtype=jnp.int32)[:, None] * ROWS_DEV
    return (orders.astype(jnp.int32) + starts).reshape(BATCH)


def setup_inputs(seed: int = 0) -> dict:
    arg_keys = jax.random.split(jax.random.key(seed), 4)
    return {
        "queries": draw_queries(jax.random.fold_in(arg_keys[3], 71), 0),
        "documents": draw_documents(jax.random.fold_in(arg_keys[3], 71), 0),
        "positives": draw_positives(jax.random.fold_in(arg_keys[3], 71), 0),
    }


def reference(queries, documents, positives):
    blocks = BATCH // ROWS_DEV
    query_rows = queries.astype(jnp.float32).reshape(blocks, ROWS_DEV, E)
    doc_rows = documents.astype(jnp.float32).reshape(blocks, ROWS_DEV, E)
    local_pos = (positives.reshape(blocks, ROWS_DEV) % ROWS_DEV).astype(jnp.int32)
    offsets = [0]
    for round_index in range(1, ROUNDS + 1):
        offsets.append(round_index * STRIDE)
        offsets.append(-round_index * STRIDE)

    def block_scores(offset):
        moved = jnp.roll(doc_rows, -offset, axis=0)
        return 20.0 * jnp.einsum("bie,bje->bij", query_rows, moved, precision=lax.Precision.HIGHEST)

    own_tile = block_scores(0)
    row_lse = jax.nn.logsumexp(own_tile, axis=2)
    col_lse = jax.nn.logsumexp(own_tile, axis=1)
    for offset in offsets[1:]:
        scores = block_scores(offset)
        row_lse = jnp.logaddexp(row_lse, jax.nn.logsumexp(scores, axis=2))
        col_lse = jnp.logaddexp(col_lse, jnp.roll(jax.nn.logsumexp(scores, axis=1), offset, axis=0))
    matches = jnp.arange(ROWS_DEV, dtype=jnp.int32)[None, None, :] == local_pos[:, :, None]
    positive_score = jnp.sum(jnp.where(matches, own_tile, 0.0), axis=2)
    col_at_pos = jnp.take_along_axis(col_lse, local_pos, axis=1)
    row_loss = 0.5 * (row_lse - positive_score) + 0.5 * (col_at_pos - positive_score)
    grad_queries = jnp.zeros((blocks, ROWS_DEV, E), jnp.float32)
    grad_documents = jnp.zeros((blocks, ROWS_DEV, E), jnp.float32)
    for offset in offsets:
        scores = block_scores(offset)
        col_part = jnp.roll(col_lse, -offset, axis=0)
        weights = 0.5 * (jnp.exp(scores - row_lse[:, :, None]) + jnp.exp(scores - col_part[:, None, :]))
        if offset == 0:
            weights = weights - matches.astype(jnp.float32)
        weights = lax.optimization_barrier(weights.astype(jnp.bfloat16)).astype(jnp.float32)
        moved = jnp.roll(doc_rows, -offset, axis=0)
        grad_queries = grad_queries + 20.0 * jnp.einsum("bij,bje->bie", weights, moved, precision=lax.Precision.HIGHEST)
        doc_terms = 20.0 * jnp.einsum("bij,bie->bje", weights, query_rows, precision=lax.Precision.HIGHEST)
        grad_documents = grad_documents + jnp.roll(doc_terms, offset, axis=0)
    return row_loss.reshape(BATCH), grad_queries.reshape(BATCH, E), grad_documents.reshape(BATCH, E)
```

```python
import jax
import jax.numpy as jnp
from jax import lax
from jax.experimental import pallas as pl
from jax.experimental.pallas import tpu as pltpu
from jax.sharding import PartitionSpec as P

MESH = pl.DeviceIdType.MESH
LOGIT_SCALE = 20.0
N = 384
E = 1024
C = 3
R = N // C
STRIP = 32
ROW_OFFS = (1, -1, 2, -2)
COL_OFFS = (3, -3, 6, -6)


def kernel(q_ref, d_ref, p_ref, loss_ref, gq_ref, gd_ref,
           qc, dc, s, w, lcol, prow, pcol, rrow, rcol, mrow, mcol,
           outq, outd, inq, ind, accq, accd,
           loc_sem, lse_ssem, lse_rsem, f_ssem, f_rsem, b_ssem, b_rsem, o_sem):
    me = lax.axis_index("dx") * 16 + lax.axis_index("dy")

    def dev(o):
        k = lax.rem(me + (17 * o) % 256, 256)
        return (lax.div(k, 16), lax.rem(k, 16))

    def rcopy(src, dst, ss, rs, o):
        return pltpu.make_async_remote_copy(
            src_ref=src, dst_ref=dst, send_sem=ss, recv_sem=rs,
            device_id=dev(o), device_id_type=MESH)

    own_q = pltpu.make_async_copy(q_ref, qc.at[pl.ds(N, N)], loc_sem.at[0])
    own_d = pltpu.make_async_copy(d_ref, dc.at[pl.ds(N, N)], loc_sem.at[1])
    own_q.start()
    own_d.start()

    barrier = pltpu.get_barrier_semaphore()
    for o in ROW_OFFS + COL_OFFS:
        pl.semaphore_signal(barrier, inc=1, device_id=dev(o), device_id_type=MESH)
    pl.semaphore_wait(barrier, 8)
    own_q.wait()
    own_d.wait()

    def fwd(buf, kind, side, j, o):
        slot = 0 if side == 0 else 2
        return rcopy(buf.at[pl.ds(N + j * R, R)], buf.at[pl.ds(slot * N + j * R, R)],
                     f_ssem.at[kind, side, j], f_rsem.at[kind, side, j], o)

    sends = []
    for j in range(C):
        for kind, buf, o in ((0, qc, 1), (1, dc, 3)):
            for side in (0, 1):
                cp = fwd(buf, kind, side, j, o if side == 0 else -o)
                cp.start()
                sends.append(cp)

    def score(a, b, rows, r0):
        s[pl.ds(a * N + r0, rows), pl.ds(b * N, N)] = LOGIT_SCALE * lax.dot_general(
            qc[pl.ds(a * N + r0, rows), :], dc[pl.ds(b * N, N), :],
            (((1,), (1,)), ((), ())), preferred_element_type=jnp.float32)

    score(1, 1, N, 0)
    for j in range(C):
        for side in (1, 0):
            fwd(qc, 0, side, j, 1).wait_recv()
            score(0 if side == 0 else 2, 1, R, j * R)
    for side in (1, 0):
        for j in range(C):
            fwd(dc, 1, side, j, 3).wait_recv()
        b = 0 if side == 0 else 2

        @pl.loop(0, 3)
        def _(a):
            s[pl.ds(pl.multiple_of(a * N, N), N), pl.ds(b * N, N)] = LOGIT_SCALE * lax.dot_general(
                qc[pl.ds(pl.multiple_of(a * N, N), N), :], dc[pl.ds(b * N, N), :],
                (((1,), (1,)), ((), ())), preferred_element_type=jnp.float32)

    nstrip = 3 * N // STRIP
    W3 = 3 * N

    def row_pass(i, cmax):
        rows = pl.ds(pl.multiple_of(i * STRIP, STRIP), STRIP)
        x = s[rows, :]
        m = jnp.max(x, axis=1, keepdims=True)
        t = jnp.sum(jnp.exp(x - m), axis=1, keepdims=True)
        lcol[rows, :] = jnp.broadcast_to(m + jnp.log(t), (STRIP, 128))
        return jnp.maximum(cmax, jnp.max(x.reshape(STRIP // 8, 8, W3), axis=0))

    cmax = lax.fori_loop(0, nstrip, row_pass, jnp.full((8, W3), -jnp.inf, jnp.float32))
    cmax = jnp.max(cmax, axis=0, keepdims=True)

    def col_pass(i, acc):
        rows = pl.ds(pl.multiple_of(i * STRIP, STRIP), STRIP)
        e = jnp.exp(s[rows, :] - cmax)
        return acc + jnp.sum(e.reshape(STRIP // 8, 8, W3), axis=0)

    csum = lax.fori_loop(0, nstrip, col_pass, jnp.zeros((8, W3), jnp.float32))
    clse = cmax + jnp.log(jnp.sum(csum, axis=0, keepdims=True))
    for b in range(3):
        pcol[b:b + 1, :] = clse[:, b * N:(b + 1) * N]
        prow[b:b + 1, :] = lcol[b * N:(b + 1) * N, :].T[0:1, :]
    prow[3:8, :] = jnp.zeros((5, N), jnp.float32)
    pcol[3:8, :] = jnp.zeros((5, N), jnp.float32)

    lse_copies = []
    for g, (part, got, offs) in enumerate(((prow, rrow, ROW_OFFS), (pcol, rcol, COL_OFFS))):
        for i, o in enumerate(offs):
            cp = rcopy(part, got.at[i], lse_ssem.at[g, i], lse_rsem.at[g, i], -o)
            cp.start()
            lse_copies.append(cp)
    for cp in lse_copies:
        cp.wait_recv()

    def merge(part, got, out):
        def lae3(x, y, z):
            m = jnp.maximum(jnp.maximum(x, y), z)
            return m + jnp.log(jnp.exp(x - m) + jnp.exp(y - m) + jnp.exp(z - m))
        out[0:1, :] = lae3(part[0:1, :], got[1, 1:2, :], got[3, 2:3, :])
        out[1:2, :] = lae3(part[1:2, :], got[0, 0:1, :], got[1, 2:3, :])
        out[2:3, :] = lae3(part[2:3, :], got[0, 1:2, :], got[2, 0:1, :])

    merge(prow, rrow, mrow)
    merge(pcol, rcol, mcol)
    for a in range(3):
        lcol[a * N:(a + 1) * N, :] = jnp.broadcast_to(mrow[a:a + 1, :], (128, N)).T
    pos = lax.rem(p_ref[0:1, :], N).astype(jnp.float32)
    accq[:, 0:128] = jnp.broadcast_to(pos, (128, N)).T

    def weights(a):
        @pl.loop(0, N // STRIP)
        def _(i):
            r0 = pl.multiple_of(i * STRIP, STRIP)
            rows = pl.ds(a * N + r0, STRIP)
            rl = lcol[rows, 0:1]
            for b in range(3):
                x = s[rows, b * N:(b + 1) * N]
                v = 0.5 * (jnp.exp(x - rl) + jnp.exp(x - mcol[b:b + 1, :]))
                if a == 1 and b == 1:
                    local = accq[pl.ds(r0, STRIP), 0:1].astype(jnp.int32)
                    hit = lax.broadcasted_iota(jnp.int32, (STRIP, N), 1) == local
                    v = v - hit.astype(jnp.float32)
                    score_at = jnp.sum(jnp.where(hit, x, 0.0), axis=1, keepdims=True)
                    col_at = jnp.sum(jnp.where(hit, mcol[1:2, :], 0.0), axis=1, keepdims=True)
                    loss = 0.5 * (rl - score_at) + 0.5 * (col_at - score_at)
                    accd[pl.ds(r0, STRIP), 0:128] = jnp.broadcast_to(loss, (STRIP, 128))
                w[rows, b * N:(b + 1) * N] = v.astype(jnp.bfloat16)

    def row_product(a, out):
        @pl.loop(0, E // 256)
        def _(n):
            cols = pl.ds(pl.multiple_of(n * 256, 256), 256)
            out[:, cols] = jnp.dot(w[a * N:(a + 1) * N, :], dc[:, cols],
                                   preferred_element_type=jnp.float32).astype(out.dtype)

    def col_product(b, out):
        @pl.loop(0, E // 256)
        def _(n):
            cols = pl.ds(pl.multiple_of(n * 256, 256), 256)
            out[:, cols] = lax.dot_general(
                w[:, b * N:(b + 1) * N], qc[:, cols], (((0,), (0,)), ((), ())),
                preferred_element_type=jnp.float32).astype(out.dtype)

    def back(kind, side, j, o):
        buf, got = ((outq, inq), (outd, ind))[kind]
        return rcopy(buf.at[side, pl.ds(j * R, R)], got.at[side, pl.ds(j * R, R)],
                     b_ssem.at[kind, side, j], b_rsem.at[kind, side, j], o)

    def send_back(kind, side):
        o = (1, 3)[kind]
        for j in range(C):
            cp = back(kind, side, j, o if side == 1 else -o)
            cp.start()
            sends.append(cp)

    weights(2)
    row_product(2, outq.at[1])
    send_back(0, 1)
    weights(0)
    row_product(0, outq.at[0])
    send_back(0, 0)
    weights(1)
    loss_ref[0:1, :] = accd[:, 0:128].T[0:1, :]
    col_product(2, outd.at[1])
    send_back(1, 1)
    col_product(0, outd.at[0])
    send_back(1, 0)
    row_product(1, accq)
    col_product(1, accd)

    outs = []
    for kind, acc, got, res in ((0, accq, inq, gq_ref), (1, accd, ind, gd_ref)):
        for j in range(C):
            for side in (0, 1):
                back(kind, side, j, 1).wait_recv()
            rows = pl.ds(j * R, R)
            acc[rows, :] = LOGIT_SCALE * (
                acc[rows, :] + got[0, rows, :].astype(jnp.float32) + got[1, rows, :].astype(jnp.float32))
            cp = pltpu.make_async_copy(acc.at[rows], res.at[rows], o_sem.at[kind, j])
            cp.start()
            outs.append(cp)
    for cp in sends + lse_copies:
        cp.wait_send()
    for cp in outs:
        cp.wait()


def per_device(queries, documents, positives):
    f32, bf16 = jnp.float32, jnp.bfloat16
    dma = pltpu.SemaphoreType.DMA
    loss, gq, gd = pl.pallas_call(
        kernel,
        out_shape=(jax.ShapeDtypeStruct((1, N), f32),
                   jax.ShapeDtypeStruct((N, E), f32),
                   jax.ShapeDtypeStruct((N, E), f32)),
        in_specs=[pl.BlockSpec(memory_space=pl.ANY), pl.BlockSpec(memory_space=pl.ANY),
                  pl.BlockSpec(memory_space=pltpu.VMEM)],
        out_specs=(pl.BlockSpec(memory_space=pltpu.VMEM), pl.BlockSpec(memory_space=pl.ANY),
                   pl.BlockSpec(memory_space=pl.ANY)),
        scratch_shapes=[
            pltpu.VMEM((3 * N, E), bf16), pltpu.VMEM((3 * N, E), bf16),
            pltpu.VMEM((3 * N, 3 * N), f32), pltpu.VMEM((3 * N, 3 * N), bf16),
            pltpu.VMEM((3 * N, 128), f32),
            pltpu.VMEM((8, N), f32), pltpu.VMEM((8, N), f32),
            pltpu.VMEM((4, 8, N), f32), pltpu.VMEM((4, 8, N), f32),
            pltpu.VMEM((8, N), f32), pltpu.VMEM((8, N), f32),
            pltpu.VMEM((2, N, E), bf16), pltpu.VMEM((2, N, E), bf16),
            pltpu.VMEM((2, N, E), bf16), pltpu.VMEM((2, N, E), bf16),
            pltpu.VMEM((N, E), f32), pltpu.VMEM((N, E), f32),
            dma((2,)), dma((2, 4)), dma((2, 4)),
            dma((2, 2, C)), dma((2, 2, C)), dma((2, 2, C)), dma((2, 2, C)), dma((2, C)),
        ],
        compiler_params=pltpu.CompilerParams(
            collective_id=0, has_side_effects=True, vmem_limit_bytes=48 * 1024 * 1024),
        cost_estimate=pl.CostEstimate(flops=8_200_000_000, bytes_accessed=8_000_000,
                                      transcendentals=5_400_000),
    )(queries, documents, positives.reshape(1, N))
    return loss.reshape(N), gq, gd


def solution(mesh):
    return jax.shard_map(
        per_device,
        mesh=mesh,
        in_specs=(P(("dx", "dy"), None), P(("dx", "dy"), None), P(("dx", "dy"))),
        out_specs=(P(("dx", "dy")), P(("dx", "dy"), None), P(("dx", "dy"), None)),
        check_vma=False,
    )
```

```python
import jax
import jax.numpy as jnp
from jax import lax
from jax.experimental import pallas as pl
from jax.experimental.pallas import tpu as pltpu
from jax.sharding import PartitionSpec as P

MESH = pl.DeviceIdType.MESH
LOGIT_SCALE = 20.0
N = 384
E = 1024
W3 = 3 * N
C = 6
R = N // C
STRIP = 32
OFFS = (1, 3)
FWD_MODES = ((384, 128, 41060, 24673, 38937, 38938, 34340, 1537), (43590, 43622, 10377, 43173, 34852, 35345, 34197, 35092))
BACK_MODES = ((384, 384, 8292, 8801, 18457, 38937, 34368, 1537), (27221, 34918, 10385, 10373, 34065, 35353, 42261, 35348))


def spot(q, plus):
    return (q // 2) * 4 * R + plus * 2 * R + (q % 2) * R


def kernel(q_ref, d_ref, p_ref, loss_ref, gq_ref, gd_ref,
           qc, dc, s, w, lcol, part, got, full, outb, inb, rel, acc,
           loc_sem, lse_ssem, lse_rsem, f_ssem, f_rsem, g_ssem, b_ssem, b_rsem, r_ssem, r_rsem, o_sem):
    me = lax.axis_index("dx") * 16 + lax.axis_index("dy")
    ring = lax.rem(me * 241, 256)
    cat = (qc, dc)
    src = (q_ref, d_ref)

    def dev(o):
        k = lax.rem(me + (17 * o) % 256, 256)
        return (lax.div(k, 16), lax.rem(k, 16))

    def mode_of(words, o):
        t = lax.rem(ring + (o % 64), 64)
        hi, lo = lax.div(t, 8), lax.rem(t, 8)
        word = jnp.int32(0)
        for i, v in enumerate(words):
            word = jnp.where(hi == i, jnp.int32(v), word)
        out = jnp.int32(0)
        for i in range(8):
            out = jnp.where(lo == i, lax.rem(lax.div(word, jnp.int32(4 ** i)), 4), out)
        return out

    def rcopy(a, b, ss, rs, o):
        return pltpu.make_async_remote_copy(
            src_ref=a, dst_ref=b, send_sem=ss, recv_sem=rs,
            device_id=dev(o), device_id_type=MESH)

    own = [pltpu.make_async_copy(src[k], cat[k].at[pl.ds(0, N)], loc_sem.at[k]) for k in (0, 1)]
    for cp in own:
        cp.start()

    barrier = pltpu.get_barrier_semaphore()
    for o in (1, -1, 2, -2, 3, -3, 6, -6):
        pl.semaphore_signal(barrier, inc=1, device_id=dev(o), device_id_type=MESH)
    fmode = [[mode_of(FWD_MODES[k], d * OFFS[k]) for d in (-1, 1, 0)] for k in (0, 1)]
    bmode = [[mode_of(BACK_MODES[k], d * OFFS[k]) for d in (-1, 1, 0)] for k in (0, 1)]
    pl.semaphore_wait(barrier, 8)

    def slot(k, plus, q):
        return cat[k].at[pl.ds(N + spot(q, plus), R)]

    def send(k, plus, q):
        o = OFFS[k] if plus == 0 else -OFFS[k]
        return rcopy(src[k].at[pl.ds(q * R, R)], slot(k, plus, q),
                     f_ssem.at[k, plus, q], f_rsem.at[k, plus, q], o)

    def forward(k, plus, q):
        o = -2 * OFFS[k] if plus == 0 else 2 * OFFS[k]
        return rcopy(slot(k, plus, q), slot(k, 1 - plus, q),
                     g_ssem.at[k, plus, q], f_rsem.at[k, 1 - plus, q], o)

    def relays(k, plus):
        return fmode[k][plus] == (1 if plus == 0 else 2)

    def sends_to(k, plus):
        return fmode[k][2] != (2 if plus == 0 else 1)

    for q in range(C):
        for k in (0, 1):
            for plus in (0, 1):
                @pl.when(sends_to(k, plus))
                def _():
                    send(k, plus, q).start()

    def pass_on(q):
        for k in (0, 1):
            for plus in (0, 1):
                @pl.when(relays(k, plus))
                def _():
                    send(k, plus, q).wait_recv()
                    forward(k, plus, q).start()

    def take(q):
        for k in (0, 1):
            for plus in (0, 1):
                @pl.when(jnp.logical_not(relays(k, plus)))
                def _():
                    send(k, plus, q).wait_recv()

    for cp in own:
        cp.wait()

    def score(g, r0, r1, c0, c1):
        s[g, r0:r1, c0:c1] = LOGIT_SCALE * lax.dot_general(
            cat[g][r0:r1, :], cat[1 - g][c0:c1, :],
            (((1,), (1,)), ((), ())), preferred_element_type=jnp.float32)

    def log_sum(g, r0, r1, c0, c1):
        n = c1 - c0
        steps = (r1 - r0) // STRIP

        def strip(i):
            return s[g, pl.ds(pl.multiple_of(r0 + i * STRIP, STRIP), STRIP), c0:c1]

        def top(i, m):
            return jnp.maximum(m, jnp.max(strip(i).reshape(STRIP // 8, 8, n), axis=0))

        m = lax.fori_loop(0, steps, top, jnp.full((8, n), -jnp.inf, jnp.float32))
        m = jnp.max(m, axis=0, keepdims=True)

        def add(i, t):
            return t + jnp.sum(jnp.exp(strip(i) - m).reshape(STRIP // 8, 8, n), axis=0)

        t = lax.fori_loop(0, steps, add, jnp.zeros((8, n), jnp.float32))
        return m + jnp.log(jnp.sum(t, axis=0, keepdims=True))

    def scores_step(j):
        base = N + j * 4 * R if j >= 0 else 0
        end = base + 4 * R if j >= 0 else N
        for g in (0, 1):
            score(g, base, end, 0, end)
            if j >= 0:
                score(g, 0, base, base, end)
        for g in (0, 1):
            if j >= 0:
                x = part[g, :, 0:base]
                y = log_sum(g, base, end, 0, base)
                m = jnp.maximum(x, y)
                part[g, :, 0:base] = m + jnp.log(jnp.exp(x - m) + jnp.exp(y - m))
            part[g, :, base:end] = log_sum(g, 0, end, base, end)

    scores_step(-1)
    for q in range(3):
        pass_on(q)
    take(0)
    take(1)
    scores_step(0)
    pass_on(3)
    pass_on(4)
    take(2)
    take(3)
    scores_step(1)
    pass_on(5)
    take(4)
    take(5)
    scores_step(2)

    lse_copies = []
    for g in (0, 1):
        for i, d in enumerate((1, -1, 2, -2)):
            cp = rcopy(part.at[g], got.at[g, i], lse_ssem.at[g, i], lse_rsem.at[g, i], -d * OFFS[1 - g])
            cp.start()
            lse_copies.append(cp)
    for cp in lse_copies:
        cp.wait_recv()

    def lae3(x, y, z):
        m = jnp.maximum(jnp.maximum(x, y), z)
        return m + jnp.log(jnp.exp(x - m) + jnp.exp(y - m) + jnp.exp(z - m))

    for g in (0, 1):
        for j in range(3):
            o, b, a = 128 * j, N + 256 * j, N + 256 * j + 128
            mine, up, down, up2, down2 = part.at[g], got.at[g, 0], got.at[g, 1], got.at[g, 2], got.at[g, 3]
            full[g, :, o:o + 128] = lae3(mine[:, o:o + 128], up[:, b:b + 128], down[:, a:a + 128])
            full[g, :, a:a + 128] = lae3(mine[:, a:a + 128], up[:, o:o + 128], up2[:, b:b + 128])
            full[g, :, b:b + 128] = lae3(mine[:, b:b + 128], down[:, o:o + 128], down2[:, a:a + 128])
    for g in (0, 1):
        for i in range(9):
            lcol[g, i * 128:(i + 1) * 128, :] = jnp.broadcast_to(
                full[1 - g, :, i * 128:(i + 1) * 128], (128, 128)).T

    def weigh(g, rows):
        x = s[g, rows, :]
        return x, 0.5 * (jnp.exp(x - lcol[g, rows, 0:1]) + jnp.exp(x - full[g]))

    def weights(g, r0, r1):
        @pl.loop(0, (r1 - r0) // STRIP)
        def _(i):
            rows = pl.ds(pl.multiple_of(r0 + i * STRIP, STRIP), STRIP)
            w[g, rows, :] = weigh(g, rows)[1].astype(jnp.bfloat16)

    def product(g, r0, rows, out, o0):
        @pl.loop(0, E // 256)
        def _(n):
            cols = pl.ds(pl.multiple_of(n * 256, 256), 256)
            out[o0:o0 + rows, cols] = jnp.dot(
                w[g, r0:r0 + rows, :], cat[1 - g][:, cols],
                preferred_element_type=jnp.float32).astype(out.dtype)

    def give(k, plus, q):
        o = OFFS[k] if plus == 1 else -OFFS[k]
        return rcopy(outb.at[k, pl.ds(spot(q, plus), R)], inb.at[k, pl.ds(spot(q, 1 - plus), R)],
                     b_ssem.at[k, plus, q], b_rsem.at[k, 1 - plus, q], o)

    def lend(k, plus, q):
        o = 2 * OFFS[k] if plus == 1 else -2 * OFFS[k]
        return rcopy(outb.at[k, pl.ds(spot(q, plus), R)], rel.at[k, pl.ds(spot(q, 1 - plus), R)],
                     r_ssem.at[k, plus, q], r_rsem.at[k, 1 - plus, q], o)

    def is_star(k, plus):
        return bmode[k][plus] == 0

    def is_leaf(k, plus):
        return bmode[k][plus] == (1 if plus == 1 else 2)

    def is_relay(k, plus):
        return bmode[k][plus] == (2 if plus == 1 else 1)

    for k in (0, 1):
        for j in range(3):
            weights(k, N + 256 * j, N + 256 * j + 256)
            product(k, N + 256 * j, 256, outb.at[k], 256 * j)
            for q in (2 * j, 2 * j + 1):
                for plus in (0, 1):
                    @pl.when(is_leaf(k, plus))
                    def _():
                        lend(k, plus, q).start()

                    @pl.when(is_star(k, plus))
                    def _():
                        give(k, plus, q).start()

    def relay_back(k, q):
        for plus in (0, 1):
            @pl.when(is_relay(k, plus))
            def _():
                lend(k, 1 - plus, q).wait_recv()
                rows = pl.ds(spot(q, plus), R)
                outb[k, rows, :] = (outb[k, rows, :].astype(jnp.float32)
                                    + rel[k, rows, :].astype(jnp.float32)).astype(jnp.bfloat16)
                give(k, plus, q).start()

    for q in range(C):
        relay_back(0, q)

    weights(1, 0, N)
    weights(0, 0, N)
    pos = lax.rem(p_ref[...], N)
    acc[0, 0:N, 0:128] = jnp.broadcast_to(pos.astype(jnp.float32), (128, N)).T
    hit = lax.broadcasted_iota(jnp.int32, (N, N), 0) == pos
    x = s[1, 0:N, 0:N]
    score_at = jnp.sum(jnp.where(hit, x, 0.0), axis=0, keepdims=True)
    col_at = jnp.sum(jnp.where(hit, lcol[1, 0:N, 0:1], 0.0), axis=0, keepdims=True)
    loss_ref[...] = 0.5 * (full[1, :, 0:N] - score_at) + 0.5 * (col_at - score_at)

    @pl.loop(0, N // STRIP)
    def _(i):
        rows = pl.ds(pl.multiple_of(i * STRIP, STRIP), STRIP)
        iota0 = lax.broadcasted_iota(jnp.int32, (STRIP, N), 0) + i * STRIP
        iota1 = lax.broadcasted_iota(jnp.int32, (STRIP, N), 1)
        at = acc[0, rows, 0:1].astype(jnp.int32)
        for g, match in ((0, iota1 == at), (1, iota0 == pos)):
            x = s[g, rows, 0:N]
            v = 0.5 * (jnp.exp(x - lcol[g, rows, 0:1]) + jnp.exp(x - full[g, :, 0:N]))
            w[g, rows, 0:N] = (v - match.astype(jnp.float32)).astype(jnp.bfloat16)

    for q in range(C):
        relay_back(1, q)
    product(0, 0, N, acc.at[0], 0)
    product(1, 0, N, acc.at[1], 0)

    outs = []
    for k, res in ((0, gq_ref), (1, gd_ref)):
        for q in range(C):
            rows = pl.ds(q * R, R)
            lo, hi = pl.ds(spot(q, 0), R), pl.ds(spot(q, 1), R)

            @pl.when(bmode[k][2] != 1)
            def _():
                give(k, 1, q).wait_recv()
                acc[k, rows, :] = acc[k, rows, :] + inb[k, lo, :].astype(jnp.float32)

            @pl.when(bmode[k][2] != 2)
            def _():
                give(k, 0, q).wait_recv()
                acc[k, rows, :] = acc[k, rows, :] + inb[k, hi, :].astype(jnp.float32)

            acc[k, rows, :] = LOGIT_SCALE * acc[k, rows, :]
            cp = pltpu.make_async_copy(acc.at[k, rows], res.at[rows], o_sem.at[k, q])
            cp.start()
            outs.append(cp)

    for k in (0, 1):
        for q in range(C):
            for plus in (0, 1):
                @pl.when(sends_to(k, plus))
                def _():
                    send(k, plus, q).wait_send()

                @pl.when(relays(k, plus))
                def _():
                    forward(k, plus, q).wait_send()

                @pl.when(is_leaf(k, plus))
                def _():
                    lend(k, plus, q).wait_send()

                @pl.when(jnp.logical_not(is_leaf(k, plus)))
                def _():
                    give(k, plus, q).wait_send()
    for cp in lse_copies:
        cp.wait_send()
    for cp in outs:
        cp.wait()


def per_device(queries, documents, positives):
    f32, bf16 = jnp.float32, jnp.bfloat16
    dma = pltpu.SemaphoreType.DMA
    loss, gq, gd = pl.pallas_call(
        kernel,
        out_shape=(jax.ShapeDtypeStruct((1, N), f32),
                   jax.ShapeDtypeStruct((N, E), f32),
                   jax.ShapeDtypeStruct((N, E), f32)),
        in_specs=[pl.BlockSpec(memory_space=pl.ANY), pl.BlockSpec(memory_space=pl.ANY),
                  pl.BlockSpec(memory_space=pltpu.VMEM)],
        out_specs=(pl.BlockSpec(memory_space=pltpu.VMEM), pl.BlockSpec(memory_space=pl.ANY),
                   pl.BlockSpec(memory_space=pl.ANY)),
        scratch_shapes=[
            pltpu.VMEM((W3, E), bf16), pltpu.VMEM((W3, E), bf16),
            pltpu.VMEM((2, W3, W3), f32), pltpu.VMEM((2, W3, W3), bf16),
            pltpu.VMEM((2, W3, 128), f32),
            pltpu.VMEM((2, 1, W3), f32), pltpu.VMEM((2, 4, 1, W3), f32), pltpu.VMEM((2, 1, W3), f32),
            pltpu.VMEM((2, 2 * N, E), bf16), pltpu.VMEM((2, 2 * N, E), bf16), pltpu.VMEM((2, 2 * N, E), bf16),
            pltpu.VMEM((2, N, E), f32),
            dma((2,)), dma((2, 4)), dma((2, 4)),
            dma((2, 2, C)), dma((2, 2, C)), dma((2, 2, C)), dma((2, 2, C)), dma((2, 2, C)),
            dma((2, 2, C)), dma((2, 2, C)), dma((2, C)),
        ],
        compiler_params=pltpu.CompilerParams(
            collective_id=0, has_side_effects=True, vmem_limit_bytes=60 * 1024 * 1024),
        cost_estimate=pl.CostEstimate(flops=11_000_000_000, bytes_accessed=8_000_000,
                                      transcendentals=11_000_000),
    )(queries, documents, positives.reshape(1, N))
    return loss.reshape(N), gq, gd


def solution(mesh):
    return jax.shard_map(
        per_device,
        mesh=mesh,
        in_specs=(P(("dx", "dy"), None), P(("dx", "dy"), None), P(("dx", "dy"))),
        out_specs=(P(("dx", "dy")), P(("dx", "dy"), None), P(("dx", "dy"), None)),
        check_vma=False,
    )
```

```python
import jax
import jax.numpy as jnp
from jax import lax
from jax.experimental import pallas as pl
from jax.experimental.pallas import tpu as pltpu
from jax.sharding import PartitionSpec as P

MESH = pl.DeviceIdType.MESH
LOGIT_SCALE = 20.0
N = 384
E = 1024
W3 = 3 * N
C = 6
R = N // C
STRIP = 32
ORDER = ((1, 0), (1, 1), (0, 0), (0, 1), (1, 2), (1, 3), (0, 2), (0, 3), (1, 4), (1, 5), (0, 4), (0, 5))
OFFS = (1, 3)
FWD_MODES = ((8584, 130, 70, 33, 38937, 38937, 33792, 514), (27206, 41494, 10256, 10400, 34833, 10256, 33045, 32788))
BACK_MODES = ((16512, 0, 512, 96, 34840, 4113, 1024, 4), (32833, 43521, 2180, 8577, 2321, 2194, 42244, 16))


def spot(q, plus):
    return (q // 2) * 4 * R + plus * 2 * R + (q % 2) * R


def kernel(q_ref, d_ref, p_ref, loss_ref, accq_ref, accd_ref, inq_ref, ind_ref,
           qc, dc, s, w, lcol, part, got, full, outb, rel, acc,
           loc_sem, lse_ssem, lse_rsem, f_ssem, f_rsem, g_ssem, b_ssem, b_rsem, r_ssem, r_rsem, o_sem, z_sem):
    me = lax.axis_index("dx") * 16 + lax.axis_index("dy")
    ring = lax.rem(me * 241, 256)
    cat = (qc, dc)
    src = (q_ref, d_ref)
    inb = (inq_ref, ind_ref)

    def dev(o):
        k = lax.rem(me + (17 * o) % 256, 256)
        return (lax.div(k, 16), lax.rem(k, 16))

    def mode_of(words, o):
        t = lax.rem(ring + (o % 64), 64)
        hi, lo = lax.div(t, 8), lax.rem(t, 8)
        word = jnp.int32(0)
        for i, v in enumerate(words):
            word = jnp.where(hi == i, jnp.int32(v), word)
        out = jnp.int32(0)
        for i in range(8):
            out = jnp.where(lo == i, lax.rem(lax.div(word, jnp.int32(4 ** i)), 4), out)
        return out

    def rcopy(a, b, ss, rs, o):
        return pltpu.make_async_remote_copy(
            src_ref=a, dst_ref=b, send_sem=ss, recv_sem=rs,
            device_id=dev(o), device_id_type=MESH)

    own = [pltpu.make_async_copy(src[k], cat[k].at[pl.ds(0, N)], loc_sem.at[k]) for k in (0, 1)]
    for cp in own:
        cp.start()

    barrier = pltpu.get_barrier_semaphore()
    for o in (1, -1, 2, -2, 3, -3, 6, -6):
        pl.semaphore_signal(barrier, inc=1, device_id=dev(o), device_id_type=MESH)
    fmode = [[mode_of(FWD_MODES[k], d * OFFS[k]) for d in (-1, 1, 0)] for k in (0, 1)]
    bmode = [[mode_of(BACK_MODES[k], d * OFFS[k]) for d in (-1, 1, 0)] for k in (0, 1)]
    pl.semaphore_wait(barrier, 8)

    def slot(k, plus, q):
        return cat[k].at[pl.ds(N + spot(q, plus), R)]

    def send(k, plus, q):
        o = OFFS[k] if plus == 0 else -OFFS[k]
        return rcopy(src[k].at[pl.ds(q * R, R)], slot(k, plus, q),
                     f_ssem.at[k, plus, q], f_rsem.at[k, plus, q], o)

    def forward(k, plus, q):
        o = -2 * OFFS[k] if plus == 0 else 2 * OFFS[k]
        return rcopy(slot(k, plus, q), slot(k, 1 - plus, q),
                     g_ssem.at[k, plus, q], f_rsem.at[k, 1 - plus, q], o)

    def relays(k, plus):
        return fmode[k][plus] == (1 if plus == 0 else 2)

    def sends_to(k, plus):
        return fmode[k][2] != (2 if plus == 0 else 1)

    for k, q in ORDER:
        for plus in (0, 1):
            @pl.when(sends_to(k, plus))
            def _():
                send(k, plus, q).start()

    def pass_on(k, q):
        for plus in (0, 1):
            @pl.when(relays(k, plus))
            def _():
                send(k, plus, q).wait_recv()
                forward(k, plus, q).start()

    def take(k, q):
        for plus in (0, 1):
            @pl.when(jnp.logical_not(relays(k, plus)))
            def _():
                send(k, plus, q).wait_recv()

    for cp in own:
        cp.wait()

    def score(g, r0, r1, c0, c1):
        s[g, r0:r1, c0:c1] = LOGIT_SCALE * lax.dot_general(
            cat[g][r0:r1, :], cat[1 - g][c0:c1, :],
            (((1,), (1,)), ((), ())), preferred_element_type=jnp.float32)

    def log_sum(g, r0, r1, c0, c1):
        n = c1 - c0
        steps = (r1 - r0) // STRIP

        def strip(i):
            return s[g, pl.ds(pl.multiple_of(r0 + i * STRIP, STRIP), STRIP), c0:c1]

        def top(i, m):
            return jnp.maximum(m, jnp.max(strip(i).reshape(STRIP // 8, 8, n), axis=0))

        m = lax.fori_loop(0, steps, top, jnp.full((8, n), -jnp.inf, jnp.float32))
        m = jnp.max(m, axis=0, keepdims=True)

        def add(i, t):
            return t + jnp.sum(jnp.exp(strip(i) - m).reshape(STRIP // 8, 8, n), axis=0)

        t = lax.fori_loop(0, steps, add, jnp.zeros((8, n), jnp.float32))
        return m + jnp.log(jnp.sum(t, axis=0, keepdims=True))

    def append(k, r0, r1, n):
        g = k
        score(g, r0, r1, 0, n)
        score(1 - g, 0, n, r0, r1)
        y = log_sum(g, r0, r1, 0, n)
        if r0 > 0:
            x = part[g, :, 0:n]
            m = jnp.maximum(x, y)
            y = m + jnp.log(jnp.exp(x - m) + jnp.exp(y - m))
        part[g, :, 0:n] = y
        part[1 - g, :, r0:r1] = log_sum(1 - g, 0, n, r0, r1)

    outb[0, 0:N, :] = jnp.zeros((N, E), jnp.bfloat16)

    def zero_side(k, plus):
        return pltpu.make_async_copy(outb.at[0, pl.ds(0, N)], inb[k].at[plus], z_sem.at[k, plus])

    for k in (0, 1):
        for plus in (0, 1):
            @pl.when(bmode[k][2] == 1 + plus)
            def _():
                zero_side(k, plus).start()

    append(0, 0, N, N)
    plan = sorted([(i, 0, k, q) for i, (k, q) in enumerate(ORDER)] + [(i + 3, 1, k, q) for i, (k, q) in enumerate(ORDER)])
    for _, late, k, q in plan:
        if not late:
            pass_on(k, q)
        else:
            take(k, q)
            if q % 2 == 1:
                base = N + (q // 2) * 4 * R
                append(k, base, base + 4 * R, base + (4 * R if k == 0 else 0))

    lse_copies = []
    for g in (0, 1):
        for i, d in enumerate((1, -1, 2, -2)):
            cp = rcopy(part.at[g], got.at[g, i], lse_ssem.at[g, i], lse_rsem.at[g, i], -d * OFFS[1 - g])
            cp.start()
            lse_copies.append(cp)
    for cp in lse_copies:
        cp.wait_recv()

    def lae3(x, y, z):
        m = jnp.maximum(jnp.maximum(x, y), z)
        return m + jnp.log(jnp.exp(x - m) + jnp.exp(y - m) + jnp.exp(z - m))

    for g in (0, 1):
        for j in range(3):
            o, b, a = 128 * j, N + 256 * j, N + 256 * j + 128
            mine, up, down, up2, down2 = part.at[g], got.at[g, 0], got.at[g, 1], got.at[g, 2], got.at[g, 3]
            full[g, :, o:o + 128] = lae3(mine[:, o:o + 128], up[:, b:b + 128], down[:, a:a + 128])
            full[g, :, a:a + 128] = lae3(mine[:, a:a + 128], up[:, o:o + 128], up2[:, b:b + 128])
            full[g, :, b:b + 128] = lae3(mine[:, b:b + 128], down[:, o:o + 128], down2[:, a:a + 128])
    def columns(g, r0, r1):
        for r in range(r0, r1, 128):
            lcol[g, r:r + 128, :] = jnp.broadcast_to(full[1 - g, :, r:r + 128], (128, 128)).T

    def weigh(g, rows):
        x = s[g, rows, :]
        return x, 0.5 * (jnp.exp(x - lcol[g, rows, 0:1]) + jnp.exp(x - full[g]))

    def weights(g, r0, r1):
        columns(g, r0, r1)

        @pl.loop(0, (r1 - r0) // STRIP)
        def _(i):
            rows = pl.ds(pl.multiple_of(r0 + i * STRIP, STRIP), STRIP)
            w[g, rows, :] = weigh(g, rows)[1].astype(jnp.bfloat16)

    def product(g, r0, rows, out, o0):
        @pl.loop(0, E // 256)
        def _(n):
            cols = pl.ds(pl.multiple_of(n * 256, 256), 256)
            out[o0:o0 + rows, cols] = jnp.dot(
                w[g, r0:r0 + rows, :], cat[1 - g][:, cols],
                preferred_element_type=jnp.float32).astype(out.dtype)

    def give(k, plus, q):
        o = OFFS[k] if plus == 1 else -OFFS[k]
        return rcopy(outb.at[k, pl.ds(spot(q, plus), R)], inb[k].at[1 - plus, pl.ds(q * R, R)],
                     b_ssem.at[k, plus, q], b_rsem.at[k, 1 - plus, q], o)

    def lend(k, plus, q):
        o = 2 * OFFS[k] if plus == 1 else -2 * OFFS[k]
        return rcopy(outb.at[k, pl.ds(spot(q, plus), R)], rel.at[k, pl.ds(spot(q, 1 - plus), R)],
                     r_ssem.at[k, plus, q], r_rsem.at[k, 1 - plus, q], o)

    def is_star(k, plus):
        return bmode[k][plus] == 0

    def is_leaf(k, plus):
        return bmode[k][plus] == (1 if plus == 1 else 2)

    def is_relay(k, plus):
        return bmode[k][plus] == (2 if plus == 1 else 1)

    for k in (0, 1):
        for plus in (0, 1):
            @pl.when(bmode[k][2] == 1 + plus)
            def _():
                zero_side(k, plus).wait()

    for k in (1, 0):
        for j in range(3):
            weights(k, N + 256 * j, N + 256 * j + 256)
            product(k, N + 256 * j, 256, outb.at[k], 256 * j)
            for q in (2 * j, 2 * j + 1):
                for plus in (0, 1):
                    @pl.when(is_leaf(k, plus))
                    def _():
                        lend(k, plus, q).start()

                    @pl.when(is_star(k, plus))
                    def _():
                        give(k, plus, q).start()

    def relay_back(k, q):
        for plus in (0, 1):
            @pl.when(is_relay(k, plus))
            def _():
                lend(k, 1 - plus, q).wait_recv()
                rows = pl.ds(spot(q, plus), R)
                outb[k, rows, :] = (outb[k, rows, :].astype(jnp.float32)
                                    + rel[k, rows, :].astype(jnp.float32)).astype(jnp.bfloat16)
                give(k, plus, q).start()

    relay_back(1, 0)
    weights(1, 0, N)
    weights(0, 0, N)
    pos = lax.rem(p_ref[...].reshape(1, N), N)
    acc[0, 0:N, 0:128] = jnp.broadcast_to(pos.astype(jnp.float32), (128, N)).T
    hit = lax.broadcasted_iota(jnp.int32, (N, N), 0) == pos
    x = s[1, 0:N, 0:N]
    score_at = jnp.sum(jnp.where(hit, x, 0.0), axis=0, keepdims=True)
    col_at = jnp.sum(jnp.where(hit, lcol[1, 0:N, 0:1], 0.0), axis=0, keepdims=True)
    loss_ref[...] = (0.5 * (full[1, :, 0:N] - score_at) + 0.5 * (col_at - score_at)).reshape(loss_ref.shape)
    relay_back(1, 1)

    @pl.loop(0, N // STRIP)
    def _(i):
        rows = pl.ds(pl.multiple_of(i * STRIP, STRIP), STRIP)
        iota0 = lax.broadcasted_iota(jnp.int32, (STRIP, N), 0) + i * STRIP
        iota1 = lax.broadcasted_iota(jnp.int32, (STRIP, N), 1)
        at = acc[0, rows, 0:1].astype(jnp.int32)
        for g, match in ((0, iota1 == at), (1, iota0 == pos)):
            x = s[g, rows, 0:N]
            v = 0.5 * (jnp.exp(x - lcol[g, rows, 0:1]) + jnp.exp(x - full[g, :, 0:N]))
            w[g, rows, 0:N] = (v - match.astype(jnp.float32)).astype(jnp.bfloat16)

    relay_back(1, 2)
    product(0, 0, N, acc.at[0], 0)
    relay_back(1, 3)
    product(1, 0, N, acc.at[1], 0)
    relay_back(1, 4)
    relay_back(1, 5)
    for q in range(C):
        relay_back(0, q)

    outs = [pltpu.make_async_copy(acc.at[k], (accq_ref, accd_ref)[k], o_sem.at[k]) for k in (0, 1)]
    for cp in outs:
        cp.start()
    for k in (1, 0):
        for q in range(C):
            @pl.when(bmode[k][2] != 1)
            def _():
                give(k, 1, q).wait_recv()

            @pl.when(bmode[k][2] != 2)
            def _():
                give(k, 0, q).wait_recv()

    for k in (0, 1):
        for q in range(C):
            for plus in (0, 1):
                @pl.when(sends_to(k, plus))
                def _():
                    send(k, plus, q).wait_send()

                @pl.when(relays(k, plus))
                def _():
                    forward(k, plus, q).wait_send()

                @pl.when(is_leaf(k, plus))
                def _():
                    lend(k, plus, q).wait_send()

                @pl.when(jnp.logical_not(is_leaf(k, plus)))
                def _():
                    give(k, plus, q).wait_send()
    for cp in lse_copies:
        cp.wait_send()
    for cp in outs:
        cp.wait()


def per_device(queries, documents, positives):
    f32, bf16 = jnp.float32, jnp.bfloat16
    dma = pltpu.SemaphoreType.DMA
    loss, accq, accd, inq, ind = pl.pallas_call(
        kernel,
        out_shape=(jax.ShapeDtypeStruct((N,), f32),
                   jax.ShapeDtypeStruct((N, E), f32),
                   jax.ShapeDtypeStruct((N, E), f32),
                   jax.ShapeDtypeStruct((2, N, E), bf16),
                   jax.ShapeDtypeStruct((2, N, E), bf16)),
        in_specs=[pl.BlockSpec(memory_space=pltpu.HBM), pl.BlockSpec(memory_space=pltpu.HBM),
                  pl.BlockSpec(memory_space=pltpu.VMEM)],
        out_specs=(pl.BlockSpec(memory_space=pltpu.VMEM),) + (pl.BlockSpec(memory_space=pl.ANY),) * 4,
        scratch_shapes=[
            pltpu.VMEM((W3, E), bf16), pltpu.VMEM((W3, E), bf16),
            pltpu.VMEM((2, W3, W3), f32), pltpu.VMEM((2, W3, W3), bf16),
            pltpu.VMEM((2, W3, 128), f32),
            pltpu.VMEM((2, 1, W3), f32), pltpu.VMEM((2, 4, 1, W3), f32), pltpu.VMEM((2, 1, W3), f32),
            pltpu.VMEM((2, 2 * N, E), bf16), pltpu.VMEM((2, 2 * N, E), bf16),
            pltpu.VMEM((2, N, E), f32),
            dma((2,)), dma((2, 4)), dma((2, 4)),
            dma((2, 2, C)), dma((2, 2, C)), dma((2, 2, C)), dma((2, 2, C)), dma((2, 2, C)),
            dma((2, 2, C)), dma((2, 2, C)), dma((2,)), dma((2, 2)),
        ],
        compiler_params=pltpu.CompilerParams(
            collective_id=0, has_side_effects=True, vmem_limit_bytes=60 * 1024 * 1024),
        cost_estimate=pl.CostEstimate(flops=11_000_000_000, bytes_accessed=8_000_000,
                                      transcendentals=11_000_000),
    )(queries, documents, positives)

    def total(a, x):
        return LOGIT_SCALE * (a + x[0].astype(f32) + x[1].astype(f32))

    return loss, total(accq, inq), total(accd, ind)


def solution(mesh):
    return jax.shard_map(
        per_device,
        mesh=mesh,
        in_specs=(P(("dx", "dy"), None), P(("dx", "dy"), None), P(("dx", "dy"))),
        out_specs=(P(("dx", "dy")), P(("dx", "dy"), None), P(("dx", "dy"), None)),
        check_vma=False,
    )
```

```python
import jax
import jax.numpy as jnp
from jax import lax
from jax.experimental import pallas as pl
from jax.experimental.pallas import tpu as pltpu
from jax.sharding import PartitionSpec as P

MESH = pl.DeviceIdType.MESH
LOGIT_SCALE = 20.0
N = 384
E = 1024
W3 = 3 * N
C = 6
R = N // C
STRIP = 32
SUM_ROWS = 48
ORDER = ((1, 0), (1, 1), (0, 0), (0, 1), (1, 2), (1, 3), (0, 2), (0, 3), (1, 4), (1, 5), (0, 4), (0, 5))
OFFS = (1, 3)
FWD_MODES = ((16768, 4480, 69, 33, 38937, 38929, 33792, 512), (26693, 41558, 10257, 10625, 2064, 10260, 1300, 20))
BACK_MODES = ((0, 10, 8192, 64, 32776, 4097, 512, 0), (32833, 33281, 2048, 8321, 2064, 2064, 33028, 16))


def spot(q, plus):
    return (q // 2) * 4 * R + plus * 2 * R + (q % 2) * R


def kernel(q_ref, d_ref, p_ref, loss_ref, accq_ref, accd_ref, inq_ref, ind_ref,
           qc, dc, s, w, lcol, part, got, full, outb, rel, acc,
           loc_sem, lse_ssem, lse_rsem, f_ssem, f_rsem, g_ssem, b_ssem, b_rsem, r_ssem, r_rsem, o_sem, z_sem):
    me = lax.axis_index("dx") * 16 + lax.axis_index("dy")
    ring = lax.rem(me * 241, 256)
    cat = (qc, dc)
    src = (q_ref, d_ref)
    inb = (inq_ref, ind_ref)

    def dev(o):
        k = lax.rem(me + (17 * o) % 256, 256)
        return (lax.div(k, 16), lax.rem(k, 16))

    def mode_of(words, o):
        t = lax.rem(ring + (o % 64), 64)
        hi, lo = lax.div(t, 8), lax.rem(t, 8)
        word = jnp.int32(0)
        for i, v in enumerate(words):
            word = jnp.where(hi == i, jnp.int32(v), word)
        out = jnp.int32(0)
        for i in range(8):
            out = jnp.where(lo == i, lax.rem(lax.div(word, jnp.int32(4 ** i)), 4), out)
        return out

    def rcopy(a, b, ss, rs, o):
        return pltpu.make_async_remote_copy(
            src_ref=a, dst_ref=b, send_sem=ss, recv_sem=rs,
            device_id=dev(o), device_id_type=MESH)

    own = [pltpu.make_async_copy(src[k], cat[k].at[pl.ds(0, N)], loc_sem.at[k]) for k in (0, 1)]
    for cp in own:
        cp.start()

    barrier = pltpu.get_barrier_semaphore()
    for o in (1, -1, 2, -2, 3, -3, 6, -6):
        pl.semaphore_signal(barrier, inc=1, device_id=dev(o), device_id_type=MESH)
    fmode = [[mode_of(FWD_MODES[k], d * OFFS[k]) for d in (-1, 1, 0)] for k in (0, 1)]
    bmode = [[mode_of(BACK_MODES[k], d * OFFS[k]) for d in (-1, 1, 0)] for k in (0, 1)]
    pl.semaphore_wait(barrier, 8)

    def slot(k, plus, q):
        return cat[k].at[pl.ds(N + spot(q, plus), R)]

    def send(k, plus, q):
        o = OFFS[k] if plus == 0 else -OFFS[k]
        return rcopy(src[k].at[pl.ds(q * R, R)], slot(k, plus, q),
                     f_ssem.at[k, plus, q], f_rsem.at[k, plus, q], o)

    def forward(k, plus, q):
        o = -2 * OFFS[k] if plus == 0 else 2 * OFFS[k]
        return rcopy(slot(k, plus, q), slot(k, 1 - plus, q),
                     g_ssem.at[k, plus, q], f_rsem.at[k, 1 - plus, q], o)

    def relays(k, plus):
        return fmode[k][plus] == (1 if plus == 0 else 2)

    def sends_to(k, plus):
        return fmode[k][2] != (2 if plus == 0 else 1)

    for k, q in ORDER:
        for plus in (0, 1):
            @pl.when(sends_to(k, plus))
            def _():
                send(k, plus, q).start()

    def pass_on(k, q):
        for plus in (0, 1):
            @pl.when(relays(k, plus))
            def _():
                send(k, plus, q).wait_recv()
                forward(k, plus, q).start()

    def take(k, q):
        for plus in (0, 1):
            @pl.when(jnp.logical_not(relays(k, plus)))
            def _():
                send(k, plus, q).wait_recv()

    for cp in own:
        cp.wait()

    def score(g, r0, r1, c0, c1):
        s[g, r0:r1, c0:c1] = LOGIT_SCALE * lax.dot_general(
            cat[g][r0:r1, :], cat[1 - g][c0:c1, :],
            (((1,), (1,)), ((), ())), preferred_element_type=jnp.float32)

    def log_sum(g, r0, r1, c0, c1):
        n = c1 - c0
        steps = (r1 - r0) // STRIP

        def strip(i):
            return s[g, pl.ds(pl.multiple_of(r0 + i * STRIP, STRIP), STRIP), c0:c1]

        def top(i, m):
            return jnp.maximum(m, jnp.max(strip(i).reshape(STRIP // 8, 8, n), axis=0))

        m = lax.fori_loop(0, steps, top, jnp.full((8, n), -jnp.inf, jnp.float32))
        m = jnp.max(m, axis=0, keepdims=True)

        def add(i, t):
            return t + jnp.sum(jnp.exp(strip(i) - m).reshape(STRIP // 8, 8, n), axis=0)

        t = lax.fori_loop(0, steps, add, jnp.zeros((8, n), jnp.float32))
        return m + jnp.log(jnp.sum(t, axis=0, keepdims=True))

    def append(k, r0, r1, n):
        g = k
        score(g, r0, r1, 0, n)
        score(1 - g, 0, n, r0, r1)
        y = log_sum(g, r0, r1, 0, n)
        if r0 > 0:
            x = part[g, :, 0:n]
            m = jnp.maximum(x, y)
            y = m + jnp.log(jnp.exp(x - m) + jnp.exp(y - m))
        part[g, :, 0:n] = y
        part[1 - g, :, r0:r1] = log_sum(1 - g, 0, n, r0, r1)

    outb[0, 0:N, :] = jnp.zeros((N, E), jnp.bfloat16)

    def zero_side(k, plus):
        return pltpu.make_async_copy(outb.at[0, pl.ds(0, N)], inb[k].at[plus], z_sem.at[k, plus])

    for k in (0, 1):
        for plus in (0, 1):
            @pl.when(bmode[k][2] == 1 + plus)
            def _():
                zero_side(k, plus).start()

    append(0, 0, N, N)
    plan = sorted([(i, 0, k, q) for i, (k, q) in enumerate(ORDER)] + [(i + 3, 1, k, q) for i, (k, q) in enumerate(ORDER)])
    for _, late, k, q in plan:
        if not late:
            pass_on(k, q)
        else:
            take(k, q)
            if q % 2 == 1:
                base = N + (q // 2) * 4 * R
                append(k, base, base + 4 * R, base + (4 * R if k == 0 else 0))

    lse_copies = []
    for g in (0, 1):
        for i, d in enumerate((1, -1, 2, -2)):
            cp = rcopy(part.at[g], got.at[g, i], lse_ssem.at[g, i], lse_rsem.at[g, i], -d * OFFS[1 - g])
            cp.start()
            lse_copies.append(cp)
    for cp in lse_copies:
        cp.wait_recv()

    def lae3(x, y, z):
        m = jnp.maximum(jnp.maximum(x, y), z)
        return m + jnp.log(jnp.exp(x - m) + jnp.exp(y - m) + jnp.exp(z - m))

    for g in (0, 1):
        for j in range(3):
            o, b, a = 128 * j, N + 256 * j, N + 256 * j + 128
            mine, up, down, up2, down2 = part.at[g], got.at[g, 0], got.at[g, 1], got.at[g, 2], got.at[g, 3]
            full[g, :, o:o + 128] = lae3(mine[:, o:o + 128], up[:, b:b + 128], down[:, a:a + 128])
            full[g, :, a:a + 128] = lae3(mine[:, a:a + 128], up[:, o:o + 128], up2[:, b:b + 128])
            full[g, :, b:b + 128] = lae3(mine[:, b:b + 128], down[:, o:o + 128], down2[:, a:a + 128])
    def columns(g, r0, r1):
        for r in range(r0, r1, 128):
            lcol[g, r:r + 128, :] = jnp.broadcast_to(full[1 - g, :, r:r + 128], (128, 128)).T

    def weigh(g, rows):
        x = s[g, rows, :]
        return x, 0.5 * (jnp.exp(x - lcol[g, rows, 0:1]) + jnp.exp(x - full[g]))

    def weights(g, r0, r1):
        columns(g, r0, r1)

        @pl.loop(0, (r1 - r0) // STRIP)
        def _(i):
            rows = pl.ds(pl.multiple_of(r0 + i * STRIP, STRIP), STRIP)
            w[g, rows, :] = weigh(g, rows)[1].astype(jnp.bfloat16)

    def product(g, r0, rows, out, o0):
        @pl.loop(0, E // 256)
        def _(n):
            cols = pl.ds(pl.multiple_of(n * 256, 256), 256)
            out[o0:o0 + rows, cols] = jnp.dot(
                w[g, r0:r0 + rows, :], cat[1 - g][:, cols],
                preferred_element_type=jnp.float32).astype(out.dtype)

    def give(k, plus, q):
        o = OFFS[k] if plus == 1 else -OFFS[k]
        return rcopy(outb.at[k, pl.ds(spot(q, plus), R)], inb[k].at[1 - plus, pl.ds(q * R, R)],
                     b_ssem.at[k, plus, q], b_rsem.at[k, 1 - plus, q], o)

    def lend(k, plus, q):
        o = 2 * OFFS[k] if plus == 1 else -2 * OFFS[k]
        return rcopy(outb.at[k, pl.ds(spot(q, plus), R)], rel.at[k, pl.ds(spot(q, 1 - plus), R)],
                     r_ssem.at[k, plus, q], r_rsem.at[k, 1 - plus, q], o)

    def is_star(k, plus):
        return bmode[k][plus] == 0

    def is_leaf(k, plus):
        return bmode[k][plus] == (1 if plus == 1 else 2)

    def is_relay(k, plus):
        return bmode[k][plus] == (2 if plus == 1 else 1)

    for k in (0, 1):
        for plus in (0, 1):
            @pl.when(bmode[k][2] == 1 + plus)
            def _():
                zero_side(k, plus).wait()

    for j in range(3):
        for k in (1, 0):
            weights(k, N + 256 * j, N + 256 * j + 256)
            product(k, N + 256 * j, 256, outb.at[k], 256 * j)
            for q in (2 * j, 2 * j + 1):
                for plus in (0, 1):
                    @pl.when(is_leaf(k, plus))
                    def _():
                        lend(k, plus, q).start()

                    @pl.when(is_star(k, plus))
                    def _():
                        give(k, plus, q).start()

    def relay_back(k, q):
        for plus in (0, 1):
            @pl.when(is_relay(k, plus))
            def _():
                lend(k, 1 - plus, q).wait_recv()
                rows = pl.ds(spot(q, plus), R)
                outb[k, rows, :] = (outb[k, rows, :].astype(jnp.float32)
                                    + rel[k, rows, :].astype(jnp.float32)).astype(jnp.bfloat16)
                give(k, plus, q).start()

    relay_back(1, 0)
    relay_back(0, 0)
    weights(1, 0, N)
    weights(0, 0, N)
    pos = lax.rem(p_ref[...].reshape(1, N), N)
    acc[0, 0:N, 0:128] = jnp.broadcast_to(pos.astype(jnp.float32), (128, N)).T
    hit = lax.broadcasted_iota(jnp.int32, (N, N), 0) == pos
    x = s[1, 0:N, 0:N]
    score_at = jnp.sum(jnp.where(hit, x, 0.0), axis=0, keepdims=True)
    col_at = jnp.sum(jnp.where(hit, lcol[1, 0:N, 0:1], 0.0), axis=0, keepdims=True)
    loss_ref[...] = (0.5 * (full[1, :, 0:N] - score_at) + 0.5 * (col_at - score_at)).reshape(loss_ref.shape)
    relay_back(1, 1)
    relay_back(0, 1)

    @pl.loop(0, N // STRIP)
    def _(i):
        rows = pl.ds(pl.multiple_of(i * STRIP, STRIP), STRIP)
        iota0 = lax.broadcasted_iota(jnp.int32, (STRIP, N), 0) + i * STRIP
        iota1 = lax.broadcasted_iota(jnp.int32, (STRIP, N), 1)
        at = acc[0, rows, 0:1].astype(jnp.int32)
        for g, match in ((0, iota1 == at), (1, iota0 == pos)):
            x = s[g, rows, 0:N]
            v = 0.5 * (jnp.exp(x - lcol[g, rows, 0:1]) + jnp.exp(x - full[g, :, 0:N]))
            w[g, rows, 0:N] = (v - match.astype(jnp.float32)).astype(jnp.bfloat16)

    relay_back(1, 2)
    relay_back(0, 2)
    product(0, 0, N, acc.at[0], 0)
    relay_back(1, 3)
    relay_back(0, 3)
    product(1, 0, N, acc.at[1], 0)
    relay_back(1, 4)
    relay_back(0, 4)
    relay_back(1, 5)
    relay_back(0, 5)

    outs = [pltpu.make_async_copy(acc.at[k], (accq_ref, accd_ref)[k], o_sem.at[k]) for k in (0, 1)]
    for cp in outs:
        cp.start()
    for q in range(C):
        for k in (1, 0):
            @pl.when(bmode[k][2] != 1)
            def _():
                give(k, 1, q).wait_recv()

            @pl.when(bmode[k][2] != 2)
            def _():
                give(k, 0, q).wait_recv()

    for k in (0, 1):
        for q in range(C):
            for plus in (0, 1):
                @pl.when(sends_to(k, plus))
                def _():
                    send(k, plus, q).wait_send()

                @pl.when(relays(k, plus))
                def _():
                    forward(k, plus, q).wait_send()

                @pl.when(is_leaf(k, plus))
                def _():
                    lend(k, plus, q).wait_send()

                @pl.when(jnp.logical_not(is_leaf(k, plus)))
                def _():
                    give(k, plus, q).wait_send()
    for cp in lse_copies:
        cp.wait_send()
    for cp in outs:
        cp.wait()


def sum_kernel(loss_in, aq, ad, xq, xd, loss_out, gq, gd):
    loss_out[...] = loss_in[...]
    for a, x, g in ((aq, xq, gq), (ad, xd, gd)):
        g[...] = LOGIT_SCALE * (a[...] + x[0].astype(jnp.float32) + x[1].astype(jnp.float32))


def per_device(queries, documents, positives):
    f32, bf16 = jnp.float32, jnp.bfloat16
    dma = pltpu.SemaphoreType.DMA
    loss, accq, accd, inq, ind = pl.pallas_call(
        kernel,
        out_shape=(jax.ShapeDtypeStruct((N,), f32),
                   jax.ShapeDtypeStruct((N, E), f32),
                   jax.ShapeDtypeStruct((N, E), f32),
                   jax.ShapeDtypeStruct((2, N, E), bf16),
                   jax.ShapeDtypeStruct((2, N, E), bf16)),
        in_specs=[pl.BlockSpec(memory_space=pltpu.HBM), pl.BlockSpec(memory_space=pltpu.HBM),
                  pl.BlockSpec(memory_space=pltpu.VMEM)],
        out_specs=(pl.BlockSpec(memory_space=pltpu.VMEM),) + (pl.BlockSpec(memory_space=pl.ANY),) * 4,
        scratch_shapes=[
            pltpu.VMEM((W3, E), bf16), pltpu.VMEM((W3, E), bf16),
            pltpu.VMEM((2, W3, W3), f32), pltpu.VMEM((2, W3, W3), bf16),
            pltpu.VMEM((2, W3, 128), f32),
            pltpu.VMEM((2, 1, W3), f32), pltpu.VMEM((2, 4, 1, W3), f32), pltpu.VMEM((2, 1, W3), f32),
            pltpu.VMEM((2, 2 * N, E), bf16), pltpu.VMEM((2, 2 * N, E), bf16),
            pltpu.VMEM((2, N, E), f32),
            dma((2,)), dma((2, 4)), dma((2, 4)),
            dma((2, 2, C)), dma((2, 2, C)), dma((2, 2, C)), dma((2, 2, C)), dma((2, 2, C)),
            dma((2, 2, C)), dma((2, 2, C)), dma((2,)), dma((2, 2)),
        ],
        compiler_params=pltpu.CompilerParams(
            collective_id=0, has_side_effects=True, vmem_limit_bytes=60 * 1024 * 1024),
        cost_estimate=pl.CostEstimate(flops=11_000_000_000, bytes_accessed=8_000_000,
                                      transcendentals=11_000_000),
    )(queries, documents, positives)

    rows = pl.BlockSpec((SUM_ROWS, E), lambda i: (i, 0))
    both = pl.BlockSpec((2, SUM_ROWS, E), lambda i: (0, i, 0))
    whole = pl.BlockSpec((N,), lambda i: (0,))
    return pl.pallas_call(
        sum_kernel,
        grid=(N // SUM_ROWS,),
        out_shape=(jax.ShapeDtypeStruct((N,), f32),
                   jax.ShapeDtypeStruct((N, E), f32),
                   jax.ShapeDtypeStruct((N, E), f32)),
        in_specs=[whole, rows, rows, both, both],
        out_specs=(whole, rows, rows),
        compiler_params=pltpu.CompilerParams(vmem_limit_bytes=60 * 1024 * 1024),
    )(loss, accq, accd, inq, ind)


def solution(mesh):
    return jax.shard_map(
        per_device,
        mesh=mesh,
        in_specs=(P(("dx", "dy"), None), P(("dx", "dy"), None), P(("dx", "dy"))),
        out_specs=(P(("dx", "dy")), P(("dx", "dy"), None), P(("dx", "dy"), None)),
        check_vma=False,
    )
```

```python
import jax
import jax.numpy as jnp
from jax import lax
from jax.experimental import pallas as pl
from jax.experimental.pallas import tpu as pltpu
from jax.sharding import PartitionSpec as P

MESH = pl.DeviceIdType.MESH
LOGIT_SCALE = 20.0
N = 384
E = 1024
W3 = 3 * N
C = 12
R = N // C
Q3 = C // 3
STRIP = 32
ORDER = tuple((1, q) for q in range(Q3 // 2)) + tuple(
    x for q in range(C) for x in (((1, q + Q3 // 2),) if q + Q3 // 2 < C else ()) + ((0, q),))
OFFS = (1, 3)
FWD_MODES = ((16768, 4480, 69, 33, 38937, 38929, 33792, 512), (26693, 41558, 10257, 10625, 2064, 10260, 1300, 20))
BACK_MODES = ((0, 10, 8192, 64, 32776, 4097, 512, 0), (32833, 33281, 2048, 8321, 2064, 2064, 33028, 16))


def spot(q, plus):
    return (q // Q3) * 256 + plus * 128 + (q % Q3) * R


def kernel(q_ref, d_ref, p_ref, loss_ref, gq_ref, gd_ref,
           qc, dc, s, w, lcol, part, got, full, outb, inb, rel, acc,
           loc_sem, lse_ssem, lse_rsem, f_ssem, f_rsem, g_ssem, b_ssem, b_rsem, r_ssem, r_rsem, o_sem):
    me = lax.axis_index("dx") * 16 + lax.axis_index("dy")
    ring = lax.rem(me * 241, 256)
    cat = (qc, dc)
    src = (q_ref, d_ref)

    def dev(o):
        k = lax.rem(me + (17 * o) % 256, 256)
        return (lax.div(k, 16), lax.rem(k, 16))

    def mode_of(words, o):
        t = lax.rem(ring + (o % 64), 64)
        hi, lo = lax.div(t, 8), lax.rem(t, 8)
        word = jnp.int32(0)
        for i, v in enumerate(words):
            word = jnp.where(hi == i, jnp.int32(v), word)
        out = jnp.int32(0)
        for i in range(8):
            out = jnp.where(lo == i, lax.rem(lax.div(word, jnp.int32(4 ** i)), 4), out)
        return out

    def rcopy(a, b, ss, rs, o):
        return pltpu.make_async_remote_copy(
            src_ref=a, dst_ref=b, send_sem=ss, recv_sem=rs,
            device_id=dev(o), device_id_type=MESH)

    own = [pltpu.make_async_copy(src[k], cat[k].at[pl.ds(0, N)], loc_sem.at[k]) for k in (0, 1)]
    for cp in own:
        cp.start()

    barrier = pltpu.get_barrier_semaphore()
    for o in (1, -1, 2, -2, 3, -3, 6, -6):
        pl.semaphore_signal(barrier, inc=1, device_id=dev(o), device_id_type=MESH)
    fmode = [[mode_of(FWD_MODES[k], d * OFFS[k]) for d in (-1, 1, 0)] for k in (0, 1)]
    bmode = [[mode_of(BACK_MODES[k], d * OFFS[k]) for d in (-1, 1, 0)] for k in (0, 1)]
    pl.semaphore_wait(barrier, 8)

    def slot(k, plus, q):
        return cat[k].at[pl.ds(N + spot(q, plus), R)]

    def send(k, plus, q):
        o = OFFS[k] if plus == 0 else -OFFS[k]
        return rcopy(src[k].at[pl.ds(q * R, R)], slot(k, plus, q),
                     f_ssem.at[k, plus, q], f_rsem.at[k, plus, q], o)

    def forward(k, plus, q):
        o = -2 * OFFS[k] if plus == 0 else 2 * OFFS[k]
        return rcopy(slot(k, plus, q), slot(k, 1 - plus, q),
                     g_ssem.at[k, plus, q], f_rsem.at[k, 1 - plus, q], o)

    def relays(k, plus):
        return fmode[k][plus] == (1 if plus == 0 else 2)

    def sends_to(k, plus):
        return fmode[k][2] != (2 if plus == 0 else 1)

    for k, q in ORDER:
        for plus in (0, 1):
            @pl.when(sends_to(k, plus))
            def _():
                send(k, plus, q).start()

    def pass_on(k, q):
        for plus in (0, 1):
            @pl.when(relays(k, plus))
            def _():
                send(k, plus, q).wait_recv()
                forward(k, plus, q).start()

    def take(k, q):
        for plus in (0, 1):
            @pl.when(jnp.logical_not(relays(k, plus)))
            def _():
                send(k, plus, q).wait_recv()

    for cp in own:
        cp.wait()

    def score(g, r0, r1, c0, c1):
        s[g, r0:r1, c0:c1] = LOGIT_SCALE * lax.dot_general(
            cat[g][r0:r1, :], cat[1 - g][c0:c1, :],
            (((1,), (1,)), ((), ())), preferred_element_type=jnp.float32)

    def log_sum(g, r0, r1, c0, c1):
        n = c1 - c0
        steps = (r1 - r0) // STRIP

        def strip(i):
            return s[g, pl.ds(pl.multiple_of(r0 + i * STRIP, STRIP), STRIP), c0:c1]

        def top(i, m):
            return jnp.maximum(m, jnp.max(strip(i).reshape(STRIP // 8, 8, n), axis=0))

        m = lax.fori_loop(0, steps, top, jnp.full((8, n), -jnp.inf, jnp.float32))
        m = jnp.max(m, axis=0, keepdims=True)

        def add(i, t):
            return t + jnp.sum(jnp.exp(strip(i) - m).reshape(STRIP // 8, 8, n), axis=0)

        t = lax.fori_loop(0, steps, add, jnp.zeros((8, n), jnp.float32))
        return m + jnp.log(jnp.sum(t, axis=0, keepdims=True))

    def append(k, r0, r1, n):
        g = k
        score(g, r0, r1, 0, n)
        score(1 - g, 0, n, r0, r1)
        y = log_sum(g, r0, r1, 0, n)
        if r0 > 0:
            x = part[g, :, 0:n]
            m = jnp.maximum(x, y)
            y = m + jnp.log(jnp.exp(x - m) + jnp.exp(y - m))
        part[g, :, 0:n] = y
        part[1 - g, :, r0:r1] = log_sum(1 - g, 0, n, r0, r1)

    append(0, 0, N, N)
    plan = sorted([(i, 0, k, q) for i, (k, q) in enumerate(ORDER)] + [(i + 5, 1, k, q) for i, (k, q) in enumerate(ORDER)])
    for _, late, k, q in plan:
        if not late:
            pass_on(k, q)
        else:
            take(k, q)
            if q % Q3 == Q3 - 1:
                base = N + (q // Q3) * 256
                append(k, base, base + 256, base + (256 if k == 0 else 0))

    lse_copies = []
    for g in (0, 1):
        for i, d in enumerate((1, -1, 2, -2)):
            cp = rcopy(part.at[g], got.at[g, i], lse_ssem.at[g, i], lse_rsem.at[g, i], -d * OFFS[1 - g])
            cp.start()
            lse_copies.append(cp)
    for cp in lse_copies:
        cp.wait_recv()

    def lae3(x, y, z):
        m = jnp.maximum(jnp.maximum(x, y), z)
        return m + jnp.log(jnp.exp(x - m) + jnp.exp(y - m) + jnp.exp(z - m))

    for g in (0, 1):
        for j in range(3):
            o, b, a = 128 * j, N + 256 * j, N + 256 * j + 128
            mine, up, down, up2, down2 = part.at[g], got.at[g, 0], got.at[g, 1], got.at[g, 2], got.at[g, 3]
            full[g, :, o:o + 128] = lae3(mine[:, o:o + 128], up[:, b:b + 128], down[:, a:a + 128])
            full[g, :, a:a + 128] = lae3(mine[:, a:a + 128], up[:, o:o + 128], up2[:, b:b + 128])
            full[g, :, b:b + 128] = lae3(mine[:, b:b + 128], down[:, o:o + 128], down2[:, a:a + 128])
    def columns(g, r0, r1):
        for r in range(r0, r1, 128):
            lcol[g, r:r + 128, :] = jnp.broadcast_to(full[1 - g, :, r:r + 128], (128, 128)).T

    def weigh(g, rows):
        x = s[g, rows, :]
        return x, 0.5 * (jnp.exp(x - lcol[g, rows, 0:1]) + jnp.exp(x - full[g]))

    def weights(g, r0, r1):
        columns(g, r0, r1)

        @pl.loop(0, (r1 - r0) // STRIP)
        def _(i):
            rows = pl.ds(pl.multiple_of(r0 + i * STRIP, STRIP), STRIP)
            w[g, rows, :] = weigh(g, rows)[1].astype(jnp.bfloat16)

    def product(g, r0, rows, out, o0):
        @pl.loop(0, E // 256)
        def _(n):
            cols = pl.ds(pl.multiple_of(n * 256, 256), 256)
            out[o0:o0 + rows, cols] = jnp.dot(
                w[g, r0:r0 + rows, :], cat[1 - g][:, cols],
                preferred_element_type=jnp.float32).astype(out.dtype)

    def give(k, plus, q):
        o = OFFS[k] if plus == 1 else -OFFS[k]
        return rcopy(outb.at[k, pl.ds(spot(q, plus), R)], inb.at[k, 1 - plus, pl.ds(q * R, R)],
                     b_ssem.at[k, plus, q], b_rsem.at[k, 1 - plus, q], o)

    def lend(k, plus, q):
        o = 2 * OFFS[k] if plus == 1 else -2 * OFFS[k]
        return rcopy(outb.at[k, pl.ds(spot(q, plus), R)], rel.at[k, pl.ds(spot(q, 1 - plus), R)],
                     r_ssem.at[k, plus, q], r_rsem.at[k, 1 - plus, q], o)

    def is_star(k, plus):
        return bmode[k][plus] == 0

    def is_leaf(k, plus):
        return bmode[k][plus] == (1 if plus == 1 else 2)

    def is_relay(k, plus):
        return bmode[k][plus] == (2 if plus == 1 else 1)

    for j in range(3):
        for k in (1, 0):
            weights(k, N + 256 * j, N + 256 * j + 256)
            product(k, N + 256 * j, 256, outb.at[k], 256 * j)
            for q in range(Q3 * j, Q3 * j + Q3):
                for plus in (0, 1):
                    @pl.when(is_leaf(k, plus))
                    def _():
                        lend(k, plus, q).start()

                    @pl.when(is_star(k, plus))
                    def _():
                        give(k, plus, q).start()

    def relay_back(k, q):
        for plus in (0, 1):
            @pl.when(is_relay(k, plus))
            def _():
                lend(k, 1 - plus, q).wait_recv()
                rows = pl.ds(spot(q, plus), R)
                outb[k, rows, :] = (outb[k, rows, :].astype(jnp.float32)
                                    + rel[k, rows, :].astype(jnp.float32)).astype(jnp.bfloat16)
                give(k, plus, q).start()

    def relay_two(i):
        for q in (2 * i, 2 * i + 1):
            for k in (1, 0):
                relay_back(k, q)

    relay_two(0)
    weights(1, 0, N)
    weights(0, 0, N)
    pos = lax.rem(p_ref[...].reshape(1, N), N)
    acc[0, 0:N, 0:128] = jnp.broadcast_to(pos.astype(jnp.float32), (128, N)).T
    hit = lax.broadcasted_iota(jnp.int32, (N, N), 0) == pos
    x = s[1, 0:N, 0:N]
    score_at = jnp.sum(jnp.where(hit, x, 0.0), axis=0, keepdims=True)
    col_at = jnp.sum(jnp.where(hit, lcol[1, 0:N, 0:1], 0.0), axis=0, keepdims=True)
    loss_ref[...] = (0.5 * (full[1, :, 0:N] - score_at) + 0.5 * (col_at - score_at)).reshape(loss_ref.shape)
    relay_two(1)

    @pl.loop(0, N // STRIP)
    def _(i):
        rows = pl.ds(pl.multiple_of(i * STRIP, STRIP), STRIP)
        iota0 = lax.broadcasted_iota(jnp.int32, (STRIP, N), 0) + i * STRIP
        iota1 = lax.broadcasted_iota(jnp.int32, (STRIP, N), 1)
        at = acc[0, rows, 0:1].astype(jnp.int32)
        for g, match in ((0, iota1 == at), (1, iota0 == pos)):
            x = s[g, rows, 0:N]
            v = 0.5 * (jnp.exp(x - lcol[g, rows, 0:1]) + jnp.exp(x - full[g, :, 0:N]))
            w[g, rows, 0:N] = (v - match.astype(jnp.float32)).astype(jnp.bfloat16)

    relay_two(2)
    product(0, 0, N, acc.at[0], 0)
    relay_two(3)
    product(1, 0, N, acc.at[1], 0)
    relay_two(4)
    relay_two(5)

    outs = []
    for q in range(C):
        for k, res in ((1, gd_ref), (0, gq_ref)):
            rows = pl.ds(q * R, R)

            @pl.when(bmode[k][2] != 1)
            def _():
                give(k, 1, q).wait_recv()
                acc[k, rows, :] = acc[k, rows, :] + inb[k, 0, rows, :].astype(jnp.float32)

            @pl.when(bmode[k][2] != 2)
            def _():
                give(k, 0, q).wait_recv()
                acc[k, rows, :] = acc[k, rows, :] + inb[k, 1, rows, :].astype(jnp.float32)

            acc[k, rows, :] = LOGIT_SCALE * acc[k, rows, :]
            cp = pltpu.make_async_copy(acc.at[k, rows], res.at[rows], o_sem.at[k, q])
            cp.start()
            outs.append(cp)

    for k in (0, 1):
        for q in range(C):
            for plus in (0, 1):
                @pl.when(sends_to(k, plus))
                def _():
                    send(k, plus, q).wait_send()

                @pl.when(relays(k, plus))
                def _():
                    forward(k, plus, q).wait_send()

                @pl.when(is_leaf(k, plus))
                def _():
                    lend(k, plus, q).wait_send()

                @pl.when(jnp.logical_not(is_leaf(k, plus)))
                def _():
                    give(k, plus, q).wait_send()
    for cp in lse_copies:
        cp.wait_send()
    for cp in outs:
        cp.wait()


def per_device(queries, documents, positives):
    f32, bf16 = jnp.float32, jnp.bfloat16
    dma = pltpu.SemaphoreType.DMA
    return pl.pallas_call(
        kernel,
        out_shape=(jax.ShapeDtypeStruct((N,), f32),
                   jax.ShapeDtypeStruct((N, E), f32),
                   jax.ShapeDtypeStruct((N, E), f32)),
        in_specs=[pl.BlockSpec(memory_space=pltpu.HBM), pl.BlockSpec(memory_space=pltpu.HBM),
                  pl.BlockSpec(memory_space=pltpu.VMEM)],
        out_specs=(pl.BlockSpec(memory_space=pltpu.VMEM),) + (pl.BlockSpec(memory_space=pl.ANY),) * 2,
        scratch_shapes=[
            pltpu.VMEM((W3, E), bf16), pltpu.VMEM((W3, E), bf16),
            pltpu.VMEM((2, W3, W3), f32), pltpu.VMEM((2, W3, W3), bf16),
            pltpu.VMEM((2, W3, 128), f32),
            pltpu.VMEM((2, 1, W3), f32), pltpu.VMEM((2, 4, 1, W3), f32), pltpu.VMEM((2, 1, W3), f32),
            pltpu.VMEM((2, 2 * N, E), bf16), pltpu.VMEM((2, 2, N, E), bf16), pltpu.VMEM((2, 2 * N, E), bf16),
            pltpu.VMEM((2, N, E), f32),
            dma((2,)), dma((2, 4)), dma((2, 4)),
            dma((2, 2, C)), dma((2, 2, C)), dma((2, 2, C)), dma((2, 2, C)), dma((2, 2, C)),
            dma((2, 2, C)), dma((2, 2, C)), dma((2, C)),
        ],
        compiler_params=pltpu.CompilerParams(
            collective_id=0, has_side_effects=True, vmem_limit_bytes=60 * 1024 * 1024),
        cost_estimate=pl.CostEstimate(flops=11_000_000_000, bytes_accessed=8_000_000,
                                      transcendentals=11_000_000),
    )(queries, documents, positives)


def solution(mesh):
    return jax.shard_map(
        per_device,
        mesh=mesh,
        in_specs=(P(("dx", "dy"), None), P(("dx", "dy"), None), P(("dx", "dy"))),
        out_specs=(P(("dx", "dy")), P(("dx", "dy"), None), P(("dx", "dy"), None)),
        check_vma=False,
    )
```

```python
import jax
import jax.numpy as jnp
from jax import lax
from jax.experimental import pallas as pl
from jax.experimental.pallas import tpu as pltpu
from jax.sharding import PartitionSpec as P

MESH = pl.DeviceIdType.MESH
LOGIT_SCALE = 20.0
N = 384
E = 1024
W3 = 3 * N
C = 6
R = N // C
Q3 = C // 3
STRIP = 32
ORDER = tuple((1, q) for q in range(Q3 // 2)) + tuple(
    x for q in range(C) for x in (((1, q + Q3 // 2),) if q + Q3 // 2 < C else ()) + ((0, q),))
OFFS = (1, 3)
FWD_MODES = (
    ((0, 0, 64, 1129, 32808, 39429, 17936, 1536), (27205, 41556, 10641, 43137, 33829, 43030, 34073, 34836)),
    ((0, 2304, 2088, 33, 32897, 32785, 41984, 16896), (65, 33090, 2065, 10369, 34912, 10337, 33060, 32784)),
)
BACK_MODES = ((0, 0, 0, 0, 34824, 4105, 1024, 0), (32833, 35329, 2052, 8321, 2064, 2064, 33028, 16))


def spot(q, plus):
    return (q // Q3) * 256 + plus * 128 + (q % Q3) * R


def kernel(q_ref, d_ref, p_ref, loss_ref, gq_ref, gd_ref,
           qc, dc, s, w, lcol, part, got, full, outb, inb, rel, acc,
           loc_sem, lse_ssem, lse_rsem, f_ssem, f_rsem, g_ssem, b_ssem, b_rsem, r_ssem, r_rsem, o_sem):
    me = lax.axis_index("dx") * 16 + lax.axis_index("dy")
    ring = lax.rem(me * 241, 256)
    cat = (qc, dc)
    src = (q_ref, d_ref)

    def dev(o):
        k = lax.rem(me + (17 * o) % 256, 256)
        return (lax.div(k, 16), lax.rem(k, 16))

    def mode_of(words, o):
        t = lax.rem(ring + (o % 64), 64)
        hi, lo = lax.div(t, 8), lax.rem(t, 8)
        word = jnp.int32(0)
        for i, v in enumerate(words):
            word = jnp.where(hi == i, jnp.int32(v), word)
        out = jnp.int32(0)
        for i in range(8):
            out = jnp.where(lo == i, lax.rem(lax.div(word, jnp.int32(4 ** i)), 4), out)
        return out

    def rcopy(a, b, ss, rs, o):
        return pltpu.make_async_remote_copy(
            src_ref=a, dst_ref=b, send_sem=ss, recv_sem=rs,
            device_id=dev(o), device_id_type=MESH)

    own = [pltpu.make_async_copy(src[k], cat[k].at[pl.ds(0, N)], loc_sem.at[k]) for k in (0, 1)]
    for cp in own:
        cp.start()

    barrier = pltpu.get_barrier_semaphore()
    for o in (1, -1, 2, -2, 3, -3, 6, -6):
        pl.semaphore_signal(barrier, inc=1, device_id=dev(o), device_id_type=MESH)
    fmode = [[[mode_of(FWD_MODES[h][k], d * OFFS[k]) for d in (-1, 1, 0)] for k in (0, 1)] for h in (0, 1)]
    bmode = [[mode_of(BACK_MODES[k], d * OFFS[k]) for d in (-1, 1, 0)] for k in (0, 1)]
    pl.semaphore_wait(barrier, 8)

    def slot(k, plus, q):
        return cat[k].at[pl.ds(N + spot(q, plus), R)]

    def send(k, plus, q):
        o = OFFS[k] if plus == 0 else -OFFS[k]
        return rcopy(src[k].at[pl.ds(q * R, R)], slot(k, plus, q),
                     f_ssem.at[k, plus, q], f_rsem.at[k, plus, q], o)

    def forward(k, plus, q):
        o = -2 * OFFS[k] if plus == 0 else 2 * OFFS[k]
        return rcopy(slot(k, plus, q), slot(k, 1 - plus, q),
                     g_ssem.at[k, plus, q], f_rsem.at[k, 1 - plus, q], o)

    def relays(k, plus, q):
        return fmode[2 * q // C][k][plus] == (1 if plus == 0 else 2)

    def sends_to(k, plus, q):
        return fmode[2 * q // C][k][2] != (2 if plus == 0 else 1)

    for k, q in ORDER:
        for plus in (0, 1):
            @pl.when(sends_to(k, plus, q))
            def _():
                send(k, plus, q).start()

    def pass_on(k, q):
        for plus in (0, 1):
            @pl.when(relays(k, plus, q))
            def _():
                send(k, plus, q).wait_recv()
                forward(k, plus, q).start()

    def take(k, q):
        for plus in (0, 1):
            @pl.when(jnp.logical_not(relays(k, plus, q)))
            def _():
                send(k, plus, q).wait_recv()

    for cp in own:
        cp.wait()

    def score(g, r0, r1, c0, c1):
        s[g, r0:r1, c0:c1] = LOGIT_SCALE * lax.dot_general(
            cat[g][r0:r1, :], cat[1 - g][c0:c1, :],
            (((1,), (1,)), ((), ())), preferred_element_type=jnp.float32)

    def log_sum(g, r0, r1, c0, c1):
        n = c1 - c0
        tall = 128 if n <= 256 else 64 if n <= 640 else STRIP
        steps = (r1 - r0) // tall

        def strip(i):
            return s[g, pl.ds(pl.multiple_of(r0 + i * tall, tall), tall), c0:c1]

        def top(i, m):
            return jnp.maximum(m, jnp.max(strip(i).reshape(tall // 8, 8, n), axis=0))

        m = lax.fori_loop(0, steps, top, jnp.full((8, n), -jnp.inf, jnp.float32))
        m = jnp.max(m, axis=0, keepdims=True)

        def add(i, t):
            return t + jnp.sum(jnp.exp(strip(i) - m).reshape(tall // 8, 8, n), axis=0)

        t = lax.fori_loop(0, steps, add, jnp.zeros((8, n), jnp.float32))
        return m + jnp.log(jnp.sum(t, axis=0, keepdims=True))

    def append(k, r0, r1, n):
        g = k
        score(g, r0, r1, 0, n)
        score(1 - g, 0, n, r0, r1)
        y = log_sum(g, r0, r1, 0, n)
        if r0 > 0:
            x = part[g, :, 0:n]
            m = jnp.maximum(x, y)
            y = m + jnp.log(jnp.exp(x - m) + jnp.exp(y - m))
        part[g, :, 0:n] = y
        part[1 - g, :, r0:r1] = log_sum(1 - g, 0, n, r0, r1)

    append(0, 0, N, N)
    plan = sorted([(i, 0, k, q) for i, (k, q) in enumerate(ORDER)] + [(i + 3, 1, k, q) for i, (k, q) in enumerate(ORDER)])
    for _, late, k, q in plan:
        if not late:
            pass_on(k, q)
        else:
            take(k, q)
            if q % Q3 == Q3 - 1:
                base = N + (q // Q3) * 256
                append(k, base, base + 256, base + (256 if k == 0 else 0))

    lse_copies = []
    for g in (0, 1):
        for i, d in enumerate((1, -1, 2, -2)):
            cp = rcopy(part.at[g], got.at[g, i], lse_ssem.at[g, i], lse_rsem.at[g, i], -d * OFFS[1 - g])
            cp.start()
            lse_copies.append(cp)
    for cp in lse_copies:
        cp.wait_recv()

    def lae3(x, y, z):
        m = jnp.maximum(jnp.maximum(x, y), z)
        return m + jnp.log(jnp.exp(x - m) + jnp.exp(y - m) + jnp.exp(z - m))

    for g in (0, 1):
        for j in range(3):
            o, b, a = 128 * j, N + 256 * j, N + 256 * j + 128
            mine, up, down, up2, down2 = part.at[g], got.at[g, 0], got.at[g, 1], got.at[g, 2], got.at[g, 3]
            full[g, :, o:o + 128] = lae3(mine[:, o:o + 128], up[:, b:b + 128], down[:, a:a + 128])
            full[g, :, a:a + 128] = lae3(mine[:, a:a + 128], up[:, o:o + 128], up2[:, b:b + 128])
            full[g, :, b:b + 128] = lae3(mine[:, b:b + 128], down[:, o:o + 128], down2[:, a:a + 128])
    def columns(g, r0, r1):
        for r in range(r0, r1, 128):
            lcol[g, r:r + 128, :] = jnp.broadcast_to(full[1 - g, :, r:r + 128], (128, 128)).T

    def weigh(g, rows):
        x = s[g, rows, :]
        return x, 0.5 * (jnp.exp(x - lcol[g, rows, 0:1]) + jnp.exp(x - full[g]))

    def weights(g, r0, r1):
        columns(g, r0, r1)

        @pl.loop(0, (r1 - r0) // STRIP)
        def _(i):
            rows = pl.ds(pl.multiple_of(r0 + i * STRIP, STRIP), STRIP)
            w[g, rows, :] = weigh(g, rows)[1].astype(jnp.bfloat16)

    def product(g, r0, rows, out, o0):
        @pl.loop(0, E // 256)
        def _(n):
            cols = pl.ds(pl.multiple_of(n * 256, 256), 256)
            out[o0:o0 + rows, cols] = jnp.dot(
                w[g, r0:r0 + rows, :], cat[1 - g][:, cols],
                preferred_element_type=jnp.float32).astype(out.dtype)

    def give(k, plus, q):
        o = OFFS[k] if plus == 1 else -OFFS[k]
        return rcopy(outb.at[k, pl.ds(spot(q, plus), R)], inb.at[k, 1 - plus, pl.ds(q * R, R)],
                     b_ssem.at[k, plus, q], b_rsem.at[k, 1 - plus, q], o)

    def lend(k, plus, q):
        o = 2 * OFFS[k] if plus == 1 else -2 * OFFS[k]
        return rcopy(outb.at[k, pl.ds(spot(q, plus), R)], rel.at[k, pl.ds(spot(q, 1 - plus), R)],
                     r_ssem.at[k, plus, q], r_rsem.at[k, 1 - plus, q], o)

    def is_star(k, plus):
        return bmode[k][plus] == 0

    def is_leaf(k, plus):
        return bmode[k][plus] == (1 if plus == 1 else 2)

    def is_relay(k, plus):
        return bmode[k][plus] == (2 if plus == 1 else 1)

    for j in range(3):
        for k in (1, 0):
            weights(k, N + 256 * j, N + 256 * j + 256)
            product(k, N + 256 * j, 256, outb.at[k], 256 * j)
            for q in range(Q3 * j, Q3 * j + Q3):
                for plus in (0, 1):
                    @pl.when(is_leaf(k, plus))
                    def _():
                        lend(k, plus, q).start()

                    @pl.when(is_star(k, plus))
                    def _():
                        give(k, plus, q).start()

    def relay_back(k, q):
        for plus in (0, 1):
            @pl.when(is_relay(k, plus))
            def _():
                lend(k, 1 - plus, q).wait_recv()
                rows = pl.ds(spot(q, plus), R)
                outb[k, rows, :] = (outb[k, rows, :].astype(jnp.float32)
                                    + rel[k, rows, :].astype(jnp.float32)).astype(jnp.bfloat16)
                give(k, plus, q).start()

    def relay_both(q):
        for k in (1, 0):
            relay_back(k, q)

    relay_both(0)
    weights(1, 0, N)
    weights(0, 0, N)
    pos = lax.rem(p_ref[...].reshape(1, N), N)
    acc[0, 0:N, 0:128] = jnp.broadcast_to(pos.astype(jnp.float32), (128, N)).T
    hit = lax.broadcasted_iota(jnp.int32, (N, N), 0) == pos
    x = s[1, 0:N, 0:N]
    score_at = jnp.sum(jnp.where(hit, x, 0.0), axis=0, keepdims=True)
    col_at = jnp.sum(jnp.where(hit, lcol[1, 0:N, 0:1], 0.0), axis=0, keepdims=True)
    loss_ref[...] = (0.5 * (full[1, :, 0:N] - score_at) + 0.5 * (col_at - score_at)).reshape(loss_ref.shape)
    relay_both(1)

    @pl.loop(0, N // STRIP)
    def _(i):
        rows = pl.ds(pl.multiple_of(i * STRIP, STRIP), STRIP)
        iota0 = lax.broadcasted_iota(jnp.int32, (STRIP, N), 0) + i * STRIP
        iota1 = lax.broadcasted_iota(jnp.int32, (STRIP, N), 1)
        at = acc[0, rows, 0:1].astype(jnp.int32)
        for g, match in ((0, iota1 == at), (1, iota0 == pos)):
            x = s[g, rows, 0:N]
            v = 0.5 * (jnp.exp(x - lcol[g, rows, 0:1]) + jnp.exp(x - full[g, :, 0:N]))
            w[g, rows, 0:N] = (v - match.astype(jnp.float32)).astype(jnp.bfloat16)

    relay_both(2)
    product(0, 0, N, acc.at[0], 0)
    relay_both(3)
    product(1, 0, N, acc.at[1], 0)
    relay_both(4)
    relay_both(5)

    outs = []
    for q in range(C):
        for k, res in ((1, gd_ref), (0, gq_ref)):
            rows = pl.ds(q * R, R)

            @pl.when(bmode[k][2] != 1)
            def _():
                give(k, 1, q).wait_recv()
                acc[k, rows, :] = acc[k, rows, :] + inb[k, 0, rows, :].astype(jnp.float32)

            @pl.when(bmode[k][2] != 2)
            def _():
                give(k, 0, q).wait_recv()
                acc[k, rows, :] = acc[k, rows, :] + inb[k, 1, rows, :].astype(jnp.float32)

            acc[k, rows, :] = LOGIT_SCALE * acc[k, rows, :]
            cp = pltpu.make_async_copy(acc.at[k, rows], res.at[rows], o_sem.at[k, q])
            cp.start()
            outs.append(cp)

    for k in (0, 1):
        for q in range(C):
            for plus in (0, 1):
                @pl.when(sends_to(k, plus, q))
                def _():
                    send(k, plus, q).wait_send()

                @pl.when(relays(k, plus, q))
                def _():
                    forward(k, plus, q).wait_send()

                @pl.when(is_leaf(k, plus))
                def _():
                    lend(k, plus, q).wait_send()

                @pl.when(jnp.logical_not(is_leaf(k, plus)))
                def _():
                    give(k, plus, q).wait_send()
    for cp in lse_copies:
        cp.wait_send()
    for cp in outs:
        cp.wait()


def per_device(queries, documents, positives):
    f32, bf16 = jnp.float32, jnp.bfloat16
    dma = pltpu.SemaphoreType.DMA
    return pl.pallas_call(
        kernel,
        out_shape=(jax.ShapeDtypeStruct((N,), f32),
                   jax.ShapeDtypeStruct((N, E), f32),
                   jax.ShapeDtypeStruct((N, E), f32)),
        in_specs=[pl.BlockSpec(memory_space=pltpu.HBM), pl.BlockSpec(memory_space=pltpu.HBM),
                  pl.BlockSpec(memory_space=pltpu.VMEM)],
        out_specs=(pl.BlockSpec(memory_space=pltpu.VMEM),) + (pl.BlockSpec(memory_space=pl.ANY),) * 2,
        scratch_shapes=[
            pltpu.VMEM((W3, E), bf16), pltpu.VMEM((W3, E), bf16),
            pltpu.VMEM((2, W3, W3), f32), pltpu.VMEM((2, W3, W3), bf16),
            pltpu.VMEM((2, W3, 128), f32),
            pltpu.VMEM((2, 1, W3), f32), pltpu.VMEM((2, 4, 1, W3), f32), pltpu.VMEM((2, 1, W3), f32),
            pltpu.VMEM((2, 2 * N, E), bf16), pltpu.VMEM((2, 2, N, E), bf16), pltpu.VMEM((2, 2 * N, E), bf16),
            pltpu.VMEM((2, N, E), f32),
            dma((2,)), dma((2, 4)), dma((2, 4)),
            dma((2, 2, C)), dma((2, 2, C)), dma((2, 2, C)), dma((2, 2, C)), dma((2, 2, C)),
            dma((2, 2, C)), dma((2, 2, C)), dma((2, C)),
        ],
        compiler_params=pltpu.CompilerParams(
            collective_id=0, has_side_effects=True, vmem_limit_bytes=60 * 1024 * 1024),
        cost_estimate=pl.CostEstimate(flops=11_000_000_000, bytes_accessed=8_000_000,
                                      transcendentals=11_000_000),
    )(queries, documents, positives)


def solution(mesh):
    return jax.shard_map(
        per_device,
        mesh=mesh,
        in_specs=(P(("dx", "dy"), None), P(("dx", "dy"), None), P(("dx", "dy"))),
        out_specs=(P(("dx", "dy")), P(("dx", "dy"), None), P(("dx", "dy"), None)),
        check_vma=False,
    )
```

```python
import jax
import jax.numpy as jnp
from jax import lax
from jax.experimental import pallas as pl
from jax.experimental.pallas import tpu as pltpu
from jax.sharding import PartitionSpec as P

MESH = pl.DeviceIdType.MESH
LOGIT_SCALE = 20.0
N = 384
E = 1024
W3 = 3 * N
C = 6
R = N // C
Q3 = C // 3
STRIP = 32
ORDER = ((1, 0), (1, 1), (0, 0), (0, 1), (1, 2), (1, 3), (0, 2), (0, 3), (1, 4), (1, 5), (0, 4), (0, 5))
OFFS = (1, 3)
FWD_MODES = ((0, 0, 96, 32, 32784, 1, 0, 1536), (10821, 43076, 8209, 43169, 1045, 43040, 1045, 34820))
BACK_MODES = ((0, 128, 32768, 0, 16402, 18434, 8, 0), (22805, 41090, 8337, 43013, 34837, 43025, 21, 43012))


def spot(q, plus):
    return (q // Q3) * 256 + plus * 128 + (q % Q3) * R


def kernel(q_ref, d_ref, p_ref, loss_ref, gq_ref, gd_ref,
           qc, dc, s, w, lcol, part, got, full, outb, inb, rel, acc,
           loc_sem, lse_ssem, lse_rsem, f_ssem, f_rsem, g_ssem, b_ssem, b_rsem, r_ssem, r_rsem, o_sem):
    me = lax.axis_index("dx") * 16 + lax.axis_index("dy")
    ring = lax.rem(me * 241, 256)
    cat = (qc, dc)
    src = (q_ref, d_ref)

    def dev(o):
        k = lax.rem(me + (17 * o) % 256, 256)
        return (lax.div(k, 16), lax.rem(k, 16))

    def mode_of(words, o):
        t = lax.rem(ring + (o % 64), 64)
        hi, lo = lax.div(t, 8), lax.rem(t, 8)
        word = jnp.int32(0)
        for i, v in enumerate(words):
            word = jnp.where(hi == i, jnp.int32(v), word)
        out = jnp.int32(0)
        for i in range(8):
            out = jnp.where(lo == i, lax.rem(lax.div(word, jnp.int32(4 ** i)), 4), out)
        return out

    def rcopy(a, b, ss, rs, o):
        return pltpu.make_async_remote_copy(
            src_ref=a, dst_ref=b, send_sem=ss, recv_sem=rs,
            device_id=dev(o), device_id_type=MESH)

    own = [pltpu.make_async_copy(src[k], cat[k].at[pl.ds(0, N)], loc_sem.at[k]) for k in (0, 1)]
    for cp in own:
        cp.start()

    barrier = pltpu.get_barrier_semaphore()
    for o in (1, -1, 2, -2, 3, -3, 6, -6):
        pl.semaphore_signal(barrier, inc=1, device_id=dev(o), device_id_type=MESH)
    fmode = [[mode_of(FWD_MODES[k], d * OFFS[k]) for d in (-1, 1, 0)] for k in (0, 1)]
    bmode = [[mode_of(BACK_MODES[k], d * OFFS[k]) for d in (-1, 1, 0)] for k in (0, 1)]
    pl.semaphore_wait(barrier, 8)

    def slot(k, plus, q):
        return cat[k].at[pl.ds(N + spot(q, plus), R)]

    def send(k, plus, q):
        o = OFFS[k] if plus == 0 else -OFFS[k]
        return rcopy(src[k].at[pl.ds(q * R, R)], slot(k, plus, q),
                     f_ssem.at[k, plus, q], f_rsem.at[k, plus, q], o)

    def forward(k, plus, q):
        o = -2 * OFFS[k] if plus == 0 else 2 * OFFS[k]
        return rcopy(slot(k, plus, q), slot(k, 1 - plus, q),
                     g_ssem.at[k, plus, q], f_rsem.at[k, 1 - plus, q], o)

    def relays(k, plus):
        return fmode[k][plus] == (1 if plus == 0 else 2)

    def sends_to(k, plus):
        return fmode[k][2] != (2 if plus == 0 else 1)

    for k, q in ORDER:
        for plus in (0, 1):
            @pl.when(sends_to(k, plus))
            def _():
                send(k, plus, q).start()

    def pass_on(k, q):
        for plus in (0, 1):
            @pl.when(relays(k, plus))
            def _():
                send(k, plus, q).wait_recv()
                forward(k, plus, q).start()

    def take(k, q):
        for plus in (0, 1):
            @pl.when(jnp.logical_not(relays(k, plus)))
            def _():
                send(k, plus, q).wait_recv()

    for cp in own:
        cp.wait()

    def score(g, r0, r1, c0, c1):
        s[g, r0:r1, c0:c1] = LOGIT_SCALE * lax.dot_general(
            cat[g][r0:r1, :], cat[1 - g][c0:c1, :],
            (((1,), (1,)), ((), ())), preferred_element_type=jnp.float32)

    def log_sum(g, r0, r1, c0, c1):
        n = c1 - c0
        tall = 128 if n <= 256 else 64 if n <= 640 else STRIP
        steps = (r1 - r0) // tall

        def strip(i):
            return s[g, pl.ds(pl.multiple_of(r0 + i * tall, tall), tall), c0:c1]

        def top(i, m):
            return jnp.maximum(m, jnp.max(strip(i).reshape(tall // 8, 8, n), axis=0))

        m = lax.fori_loop(0, steps, top, jnp.full((8, n), -jnp.inf, jnp.float32))
        m = jnp.max(m, axis=0, keepdims=True)

        def add(i, t):
            return t + jnp.sum(jnp.exp(strip(i) - m).reshape(tall // 8, 8, n), axis=0)

        t = lax.fori_loop(0, steps, add, jnp.zeros((8, n), jnp.float32))
        return m + jnp.log(jnp.sum(t, axis=0, keepdims=True))

    def append(k, r0, r1, n):
        g = k
        score(g, r0, r1, 0, n)
        score(1 - g, 0, n, r0, r1)
        y = log_sum(g, r0, r1, 0, n)
        if r0 > 0:
            x = part[g, :, 0:n]
            m = jnp.maximum(x, y)
            y = m + jnp.log(jnp.exp(x - m) + jnp.exp(y - m))
        part[g, :, 0:n] = y
        part[1 - g, :, r0:r1] = log_sum(1 - g, 0, n, r0, r1)

    append(0, 0, N, N)
    plan = sorted([(i, 0, k, q) for i, (k, q) in enumerate(ORDER)] + [(i + 3, 1, k, q) for i, (k, q) in enumerate(ORDER)])
    for _, late, k, q in plan:
        if not late:
            pass_on(k, q)
        else:
            take(k, q)
            if q % Q3 == Q3 - 1:
                base = N + (q // Q3) * 256
                append(k, base, base + 256, base + (256 if k == 0 else 0))

    lse_copies = []
    for g in (0, 1):
        for i, d in enumerate((1, -1, 2, -2)):
            cp = rcopy(part.at[g], got.at[g, i], lse_ssem.at[g, i], lse_rsem.at[g, i], -d * OFFS[1 - g])
            cp.start()
            lse_copies.append(cp)
    for cp in lse_copies:
        cp.wait_recv()

    def lae3(x, y, z):
        m = jnp.maximum(jnp.maximum(x, y), z)
        return m + jnp.log(jnp.exp(x - m) + jnp.exp(y - m) + jnp.exp(z - m))

    for g in (0, 1):
        for j in range(3):
            o, b, a = 128 * j, N + 256 * j, N + 256 * j + 128
            mine, up, down, up2, down2 = part.at[g], got.at[g, 0], got.at[g, 1], got.at[g, 2], got.at[g, 3]
            full[g, :, o:o + 128] = lae3(mine[:, o:o + 128], up[:, b:b + 128], down[:, a:a + 128])
            full[g, :, a:a + 128] = lae3(mine[:, a:a + 128], up[:, o:o + 128], up2[:, b:b + 128])
            full[g, :, b:b + 128] = lae3(mine[:, b:b + 128], down[:, o:o + 128], down2[:, a:a + 128])
    def columns(g, r0, r1):
        for r in range(r0, r1, 128):
            lcol[g, r:r + 128, :] = jnp.broadcast_to(full[1 - g, :, r:r + 128], (128, 128)).T

    def weigh(g, rows):
        x = s[g, rows, :]
        return x, 0.5 * (jnp.exp(x - lcol[g, rows, 0:1]) + jnp.exp(x - full[g]))

    def weights(g, r0, r1):
        columns(g, r0, r1)

        @pl.loop(0, (r1 - r0) // STRIP)
        def _(i):
            rows = pl.ds(pl.multiple_of(r0 + i * STRIP, STRIP), STRIP)
            w[g, rows, :] = weigh(g, rows)[1].astype(jnp.bfloat16)

    def product(g, r0, rows, out, o0):
        @pl.loop(0, E // 256)
        def _(n):
            cols = pl.ds(pl.multiple_of(n * 256, 256), 256)
            out[o0:o0 + rows, cols] = jnp.dot(
                w[g, r0:r0 + rows, :], cat[1 - g][:, cols],
                preferred_element_type=jnp.float32).astype(out.dtype)

    def give(k, plus, q):
        o = OFFS[k] if plus == 1 else -OFFS[k]
        return rcopy(outb.at[k, pl.ds(spot(q, plus), R)], inb.at[k, 1 - plus, pl.ds(q * R, R)],
                     b_ssem.at[k, plus, q], b_rsem.at[k, 1 - plus, q], o)

    def lend(k, plus, q):
        o = 2 * OFFS[k] if plus == 1 else -2 * OFFS[k]
        return rcopy(outb.at[k, pl.ds(spot(q, plus), R)], rel.at[k, pl.ds(spot(q, 1 - plus), R)],
                     r_ssem.at[k, plus, q], r_rsem.at[k, 1 - plus, q], o)

    def is_star(k, plus):
        return bmode[k][plus] == 0

    def is_leaf(k, plus):
        return bmode[k][plus] == (1 if plus == 1 else 2)

    def is_relay(k, plus):
        return bmode[k][plus] == (2 if plus == 1 else 1)

    for j in range(3):
        for k in (1, 0):
            weights(k, N + 256 * j, N + 256 * j + 256)
            product(k, N + 256 * j, 256, outb.at[k], 256 * j)
            for q in range(Q3 * j, Q3 * j + Q3):
                for plus in (0, 1):
                    @pl.when(is_leaf(k, plus))
                    def _():
                        lend(k, plus, q).start()

                    @pl.when(is_star(k, plus))
                    def _():
                        give(k, plus, q).start()

    def relay_back(k, q):
        for plus in (0, 1):
            @pl.when(is_relay(k, plus))
            def _():
                lend(k, 1 - plus, q).wait_recv()
                rows = pl.ds(spot(q, plus), R)
                outb[k, rows, :] = (outb[k, rows, :].astype(jnp.float32)
                                    + rel[k, rows, :].astype(jnp.float32)).astype(jnp.bfloat16)
                give(k, plus, q).start()

    def relay_both(q):
        for k in (1, 0):
            relay_back(k, q)

    relay_both(0)
    weights(1, 0, N)
    weights(0, 0, N)
    pos = lax.rem(p_ref[...].reshape(1, N), N)
    acc[0, 0:N, 0:128] = jnp.broadcast_to(pos.astype(jnp.float32), (128, N)).T
    hit = lax.broadcasted_iota(jnp.int32, (N, N), 0) == pos
    x = s[1, 0:N, 0:N]
    score_at = jnp.sum(jnp.where(hit, x, 0.0), axis=0, keepdims=True)
    col_at = jnp.sum(jnp.where(hit, lcol[1, 0:N, 0:1], 0.0), axis=0, keepdims=True)
    loss_ref[...] = (0.5 * (full[1, :, 0:N] - score_at) + 0.5 * (col_at - score_at)).reshape(loss_ref.shape)
    relay_both(1)

    @pl.loop(0, N // STRIP)
    def _(i):
        rows = pl.ds(pl.multiple_of(i * STRIP, STRIP), STRIP)
        iota0 = lax.broadcasted_iota(jnp.int32, (STRIP, N), 0) + i * STRIP
        iota1 = lax.broadcasted_iota(jnp.int32, (STRIP, N), 1)
        at = acc[0, rows, 0:1].astype(jnp.int32)
        for g, match in ((0, iota1 == at), (1, iota0 == pos)):
            x = s[g, rows, 0:N]
            v = 0.5 * (jnp.exp(x - lcol[g, rows, 0:1]) + jnp.exp(x - full[g, :, 0:N]))
            w[g, rows, 0:N] = (v - match.astype(jnp.float32)).astype(jnp.bfloat16)

    relay_both(2)
    product(0, 0, N, acc.at[0], 0)
    relay_both(3)
    product(1, 0, N, acc.at[1], 0)
    relay_both(4)
    relay_both(5)

    outs = []
    for q in range(C):
        for k, res in ((1, gd_ref), (0, gq_ref)):
            rows = pl.ds(q * R, R)

            @pl.when(bmode[k][2] != 1)
            def _():
                give(k, 1, q).wait_recv()
                acc[k, rows, :] = acc[k, rows, :] + inb[k, 0, rows, :].astype(jnp.float32)

            @pl.when(bmode[k][2] != 2)
            def _():
                give(k, 0, q).wait_recv()
                acc[k, rows, :] = acc[k, rows, :] + inb[k, 1, rows, :].astype(jnp.float32)

            acc[k, rows, :] = LOGIT_SCALE * acc[k, rows, :]
            cp = pltpu.make_async_copy(acc.at[k, rows], res.at[rows], o_sem.at[k, q])
            cp.start()
            outs.append(cp)

    for k in (0, 1):
        for q in range(C):
            for plus in (0, 1):
                @pl.when(sends_to(k, plus))
                def _():
                    send(k, plus, q).wait_send()

                @pl.when(relays(k, plus))
                def _():
                    forward(k, plus, q).wait_send()

                @pl.when(is_leaf(k, plus))
                def _():
                    lend(k, plus, q).wait_send()

                @pl.when(jnp.logical_not(is_leaf(k, plus)))
                def _():
                    give(k, plus, q).wait_send()
    for cp in lse_copies:
        cp.wait_send()
    for cp in outs:
        cp.wait()


def per_device(queries, documents, positives):
    f32, bf16 = jnp.float32, jnp.bfloat16
    dma = pltpu.SemaphoreType.DMA
    return pl.pallas_call(
        kernel,
        out_shape=(jax.ShapeDtypeStruct((N,), f32),
                   jax.ShapeDtypeStruct((N, E), f32),
                   jax.ShapeDtypeStruct((N, E), f32)),
        in_specs=[pl.BlockSpec(memory_space=pltpu.HBM), pl.BlockSpec(memory_space=pltpu.HBM),
                  pl.BlockSpec(memory_space=pltpu.VMEM)],
        out_specs=(pl.BlockSpec(memory_space=pltpu.VMEM),) + (pl.BlockSpec(memory_space=pl.ANY),) * 2,
        scratch_shapes=[
            pltpu.VMEM((W3, E), bf16), pltpu.VMEM((W3, E), bf16),
            pltpu.VMEM((2, W3, W3), f32), pltpu.VMEM((2, W3, W3), bf16),
            pltpu.VMEM((2, W3, 128), f32),
            pltpu.VMEM((2, 1, W3), f32), pltpu.VMEM((2, 4, 1, W3), f32), pltpu.VMEM((2, 1, W3), f32),
            pltpu.VMEM((2, 2 * N, E), bf16), pltpu.VMEM((2, 2, N, E), bf16), pltpu.VMEM((2, 2 * N, E), bf16),
            pltpu.VMEM((2, N, E), f32),
            dma((2,)), dma((2, 4)), dma((2, 4)),
            dma((2, 2, C)), dma((2, 2, C)), dma((2, 2, C)), dma((2, 2, C)), dma((2, 2, C)),
            dma((2, 2, C)), dma((2, 2, C)), dma((2, C)),
        ],
        compiler_params=pltpu.CompilerParams(
            collective_id=0, has_side_effects=True, vmem_limit_bytes=60 * 1024 * 1024),
        cost_estimate=pl.CostEstimate(flops=11_000_000_000, bytes_accessed=8_000_000,
                                      transcendentals=11_000_000),
    )(queries, documents, positives)


def solution(mesh):
    return jax.shard_map(
        per_device,
        mesh=mesh,
        in_specs=(P(("dx", "dy"), None), P(("dx", "dy"), None), P(("dx", "dy"))),
        out_specs=(P(("dx", "dy")), P(("dx", "dy"), None), P(("dx", "dy"), None)),
        check_vma=False,
    )
```

```python
import jax
import jax.numpy as jnp
from jax import lax
from jax.experimental import pallas as pl
from jax.experimental.pallas import tpu as pltpu
from jax.sharding import PartitionSpec as P

MESH = pl.DeviceIdType.MESH
LOGIT_SCALE = 20.0
N = 384
E = 1024
W3 = 3 * N
C = 6
R = N // C
Q3 = C // 3
STRIP = 32
ORDER = ((1, 0), (1, 1), (0, 0), (0, 1), (1, 2), (1, 3), (0, 2), (0, 3), (1, 4), (1, 5), (0, 4), (0, 5))
OFFS = (1, 3)
FWD_MODES = ((0, 0, 96, 32, 32784, 1, 0, 1536), (10821, 43076, 8209, 43169, 1045, 43040, 1045, 34820))
BACK_MODES = ((0, 10, 8192, 64, 32776, 4097, 512, 0), (32833, 33281, 2048, 8321, 2064, 2064, 33028, 16))


def spot(q, plus):
    return (q // Q3) * 256 + plus * 128 + (q % Q3) * R


def kernel(q_ref, d_ref, p_ref, loss_ref, gq_ref, gd_ref,
           qc, dc, s, w, lcol, part, got, full, outb, inb, rel, acc,
           loc_sem, lse_ssem, lse_rsem, f_ssem, f_rsem, g_ssem, b_ssem, b_rsem, r_ssem, r_rsem, o_sem):
    me = lax.axis_index("dx") * 16 + lax.axis_index("dy")
    ring = lax.rem(me * 241, 256)
    cat = (qc, dc)
    src = (q_ref, d_ref)

    def dev(o):
        k = lax.rem(me + (17 * o) % 256, 256)
        return (lax.div(k, 16), lax.rem(k, 16))

    def mode_of(words, o):
        t = lax.rem(ring + (o % 64), 64)
        hi, lo = lax.div(t, 8), lax.rem(t, 8)
        word = jnp.int32(0)
        for i, v in enumerate(words):
            word = jnp.where(hi == i, jnp.int32(v), word)
        out = jnp.int32(0)
        for i in range(8):
            out = jnp.where(lo == i, lax.rem(lax.div(word, jnp.int32(4 ** i)), 4), out)
        return out

    def rcopy(a, b, ss, rs, o):
        return pltpu.make_async_remote_copy(
            src_ref=a, dst_ref=b, send_sem=ss, recv_sem=rs,
            device_id=dev(o), device_id_type=MESH)

    own = [pltpu.make_async_copy(src[k], cat[k].at[pl.ds(0, N)], loc_sem.at[k]) for k in (0, 1)]
    for cp in own:
        cp.start()

    barrier = pltpu.get_barrier_semaphore()
    for o in (1, -1, 2, -2, 3, -3, 6, -6):
        pl.semaphore_signal(barrier, inc=1, device_id=dev(o), device_id_type=MESH)
    fmode = [[mode_of(FWD_MODES[k], d * OFFS[k]) for d in (-1, 1, 0)] for k in (0, 1)]
    bmode = [[mode_of(BACK_MODES[k], d * OFFS[k]) for d in (-1, 1, 0)] for k in (0, 1)]
    pl.semaphore_wait(barrier, 8)

    def slot(k, plus, q):
        return cat[k].at[pl.ds(N + spot(q, plus), R)]

    def send(k, plus, q):
        o = OFFS[k] if plus == 0 else -OFFS[k]
        return rcopy(src[k].at[pl.ds(q * R, R)], slot(k, plus, q),
                     f_ssem.at[k, plus, q], f_rsem.at[k, plus, q], o)

    def forward(k, plus, q):
        o = -2 * OFFS[k] if plus == 0 else 2 * OFFS[k]
        return rcopy(slot(k, plus, q), slot(k, 1 - plus, q),
                     g_ssem.at[k, plus, q], f_rsem.at[k, 1 - plus, q], o)

    def relays(k, plus):
        return fmode[k][plus] == (1 if plus == 0 else 2)

    def sends_to(k, plus):
        return fmode[k][2] != (2 if plus == 0 else 1)

    for k, q in ORDER:
        for plus in (0, 1):
            @pl.when(sends_to(k, plus))
            def _():
                send(k, plus, q).start()

    def pass_on(k, q):
        for plus in (0, 1):
            @pl.when(relays(k, plus))
            def _():
                send(k, plus, q).wait_recv()
                forward(k, plus, q).start()

    def take(k, q):
        for plus in (0, 1):
            @pl.when(jnp.logical_not(relays(k, plus)))
            def _():
                send(k, plus, q).wait_recv()

    for cp in own:
        cp.wait()

    def score(g, r0, r1, c0, c1):
        s[g, r0:r1, c0:c1] = LOGIT_SCALE * lax.dot_general(
            cat[g][r0:r1, :], cat[1 - g][c0:c1, :],
            (((1,), (1,)), ((), ())), preferred_element_type=jnp.float32)

    def log_sum(g, r0, r1, c0, c1):
        n = c1 - c0
        tall = 128 if n <= 256 else 64 if n <= 640 else STRIP
        steps = (r1 - r0) // tall

        def strip(i):
            return s[g, pl.ds(pl.multiple_of(r0 + i * tall, tall), tall), c0:c1]

        def top(i, m):
            return jnp.maximum(m, jnp.max(strip(i).reshape(tall // 8, 8, n), axis=0))

        m = lax.fori_loop(0, steps, top, jnp.full((8, n), -jnp.inf, jnp.float32))
        m = jnp.max(m, axis=0, keepdims=True)

        def add(i, t):
            return t + jnp.sum(jnp.exp(strip(i) - m).reshape(tall // 8, 8, n), axis=0)

        t = lax.fori_loop(0, steps, add, jnp.zeros((8, n), jnp.float32))
        return m + jnp.log(jnp.sum(t, axis=0, keepdims=True))

    def append(k, r0, r1, n):
        g = k
        score(g, r0, r1, 0, n)
        score(1 - g, 0, n, r0, r1)
        y = log_sum(g, r0, r1, 0, n)
        if r0 > 0:
            x = part[g, :, 0:n]
            m = jnp.maximum(x, y)
            y = m + jnp.log(jnp.exp(x - m) + jnp.exp(y - m))
        part[g, :, 0:n] = y
        part[1 - g, :, r0:r1] = log_sum(1 - g, 0, n, r0, r1)

    append(0, 0, N, N)
    plan = sorted([(i, 0, k, q) for i, (k, q) in enumerate(ORDER)] + [(i + 3, 1, k, q) for i, (k, q) in enumerate(ORDER)])
    for _, late, k, q in plan:
        if not late:
            pass_on(k, q)
        else:
            take(k, q)
            if q % Q3 == Q3 - 1:
                base = N + (q // Q3) * 256
                append(k, base, base + 256, base + (256 if k == 0 else 0))

    lse_copies = []
    for g in (0, 1):
        for i, d in enumerate((1, -1, 2, -2)):
            cp = rcopy(part.at[g], got.at[g, i], lse_ssem.at[g, i], lse_rsem.at[g, i], -d * OFFS[1 - g])
            cp.start()
            lse_copies.append(cp)
    for cp in lse_copies:
        cp.wait_recv()

    def lae3(x, y, z):
        m = jnp.maximum(jnp.maximum(x, y), z)
        return m + jnp.log(jnp.exp(x - m) + jnp.exp(y - m) + jnp.exp(z - m))

    for g in (0, 1):
        for j in range(3):
            o, b, a = 128 * j, N + 256 * j, N + 256 * j + 128
            mine, up, down, up2, down2 = part.at[g], got.at[g, 0], got.at[g, 1], got.at[g, 2], got.at[g, 3]
            full[g, :, o:o + 128] = lae3(mine[:, o:o + 128], up[:, b:b + 128], down[:, a:a + 128])
            full[g, :, a:a + 128] = lae3(mine[:, a:a + 128], up[:, o:o + 128], up2[:, b:b + 128])
            full[g, :, b:b + 128] = lae3(mine[:, b:b + 128], down[:, o:o + 128], down2[:, a:a + 128])
    def columns(g, r0, r1):
        for r in range(r0, r1, 128):
            lcol[g, r:r + 128, :] = jnp.broadcast_to(full[1 - g, :, r:r + 128], (128, 128)).T

    def weigh(g, rows):
        x = s[g, rows, :]
        return x, 0.5 * (jnp.exp(x - lcol[g, rows, 0:1]) + jnp.exp(x - full[g]))

    def weights(g, r0, r1):
        columns(g, r0, r1)

        @pl.loop(0, (r1 - r0) // STRIP)
        def _(i):
            rows = pl.ds(pl.multiple_of(r0 + i * STRIP, STRIP), STRIP)
            w[g, rows, :] = weigh(g, rows)[1].astype(jnp.bfloat16)

    def product(g, r0, rows, out, o0):
        @pl.loop(0, E // 256)
        def _(n):
            cols = pl.ds(pl.multiple_of(n * 256, 256), 256)
            out[o0:o0 + rows, cols] = jnp.dot(
                w[g, r0:r0 + rows, :], cat[1 - g][:, cols],
                preferred_element_type=jnp.float32).astype(out.dtype)

    def give(k, plus, q):
        o = OFFS[k] if plus == 1 else -OFFS[k]
        return rcopy(outb.at[k, pl.ds(spot(q, plus), R)], inb.at[k, 1 - plus, pl.ds(q * R, R)],
                     b_ssem.at[k, plus, q], b_rsem.at[k, 1 - plus, q], o)

    def lend(k, plus, q):
        o = 2 * OFFS[k] if plus == 1 else -2 * OFFS[k]
        return rcopy(outb.at[k, pl.ds(spot(q, plus), R)], rel.at[k, pl.ds(spot(q, 1 - plus), R)],
                     r_ssem.at[k, plus, q], r_rsem.at[k, 1 - plus, q], o)

    def is_star(k, plus):
        return bmode[k][plus] == 0

    def is_leaf(k, plus):
        return bmode[k][plus] == (1 if plus == 1 else 2)

    def is_relay(k, plus):
        return bmode[k][plus] == (2 if plus == 1 else 1)

    for j in range(3):
        for k in (1, 0):
            weights(k, N + 256 * j, N + 256 * j + 256)
            product(k, N + 256 * j, 256, outb.at[k], 256 * j)
            for q in range(Q3 * j, Q3 * j + Q3):
                for plus in (0, 1):
                    @pl.when(is_leaf(k, plus))
                    def _():
                        lend(k, plus, q).start()

                    @pl.when(is_star(k, plus))
                    def _():
                        give(k, plus, q).start()

    def relay_back(k, q):
        for plus in (0, 1):
            @pl.when(is_relay(k, plus))
            def _():
                lend(k, 1 - plus, q).wait_recv()
                rows = pl.ds(spot(q, plus), R)
                outb[k, rows, :] = (outb[k, rows, :].astype(jnp.float32)
                                    + rel[k, rows, :].astype(jnp.float32)).astype(jnp.bfloat16)
                give(k, plus, q).start()

    def relay_both(q):
        for k in (1, 0):
            relay_back(k, q)

    relay_both(0)
    weights(1, 0, N)
    weights(0, 0, N)
    pos = lax.rem(p_ref[...].reshape(1, N), N)
    acc[0, 0:N, 0:128] = jnp.broadcast_to(pos.astype(jnp.float32), (128, N)).T
    hit = lax.broadcasted_iota(jnp.int32, (N, N), 0) == pos
    x = s[1, 0:N, 0:N]
    score_at = jnp.sum(jnp.where(hit, x, 0.0), axis=0, keepdims=True)
    col_at = jnp.sum(jnp.where(hit, lcol[1, 0:N, 0:1], 0.0), axis=0, keepdims=True)
    loss_ref[...] = (0.5 * (full[1, :, 0:N] - score_at) + 0.5 * (col_at - score_at)).reshape(loss_ref.shape)
    relay_both(1)

    @pl.loop(0, N // STRIP)
    def _(i):
        rows = pl.ds(pl.multiple_of(i * STRIP, STRIP), STRIP)
        iota0 = lax.broadcasted_iota(jnp.int32, (STRIP, N), 0) + i * STRIP
        iota1 = lax.broadcasted_iota(jnp.int32, (STRIP, N), 1)
        at = acc[0, rows, 0:1].astype(jnp.int32)
        for g, match in ((0, iota1 == at), (1, iota0 == pos)):
            x = s[g, rows, 0:N]
            v = 0.5 * (jnp.exp(x - lcol[g, rows, 0:1]) + jnp.exp(x - full[g, :, 0:N]))
            w[g, rows, 0:N] = (v - match.astype(jnp.float32)).astype(jnp.bfloat16)

    relay_both(2)
    product(0, 0, N, acc.at[0], 0)
    relay_both(3)
    product(1, 0, N, acc.at[1], 0)
    relay_both(4)
    relay_both(5)

    outs = []
    for q in range(C):
        for k, res in ((1, gd_ref), (0, gq_ref)):
            rows = pl.ds(q * R, R)

            @pl.when(bmode[k][2] != 1)
            def _():
                give(k, 1, q).wait_recv()
                acc[k, rows, :] = acc[k, rows, :] + inb[k, 0, rows, :].astype(jnp.float32)

            @pl.when(bmode[k][2] != 2)
            def _():
                give(k, 0, q).wait_recv()
                acc[k, rows, :] = acc[k, rows, :] + inb[k, 1, rows, :].astype(jnp.float32)

            acc[k, rows, :] = LOGIT_SCALE * acc[k, rows, :]
            cp = pltpu.make_async_copy(acc.at[k, rows], res.at[rows], o_sem.at[k, q])
            cp.start()
            outs.append(cp)

    for k in (0, 1):
        for q in range(C):
            for plus in (0, 1):
                @pl.when(sends_to(k, plus))
                def _():
                    send(k, plus, q).wait_send()

                @pl.when(relays(k, plus))
                def _():
                    forward(k, plus, q).wait_send()

                @pl.when(is_leaf(k, plus))
                def _():
                    lend(k, plus, q).wait_send()

                @pl.when(jnp.logical_not(is_leaf(k, plus)))
                def _():
                    give(k, plus, q).wait_send()
    for cp in lse_copies:
        cp.wait_send()
    for cp in outs:
        cp.wait()


def per_device(queries, documents, positives):
    f32, bf16 = jnp.float32, jnp.bfloat16
    dma = pltpu.SemaphoreType.DMA
    return pl.pallas_call(
        kernel,
        out_shape=(jax.ShapeDtypeStruct((N,), f32),
                   jax.ShapeDtypeStruct((N, E), f32),
                   jax.ShapeDtypeStruct((N, E), f32)),
        in_specs=[pl.BlockSpec(memory_space=pltpu.HBM), pl.BlockSpec(memory_space=pltpu.HBM),
                  pl.BlockSpec(memory_space=pltpu.VMEM)],
        out_specs=(pl.BlockSpec(memory_space=pltpu.VMEM),) + (pl.BlockSpec(memory_space=pl.ANY),) * 2,
        scratch_shapes=[
            pltpu.VMEM((W3, E), bf16), pltpu.VMEM((W3, E), bf16),
            pltpu.VMEM((2, W3, W3), f32), pltpu.VMEM((2, W3, W3), bf16),
            pltpu.VMEM((2, W3, 128), f32),
            pltpu.VMEM((2, 1, W3), f32), pltpu.VMEM((2, 4, 1, W3), f32), pltpu.VMEM((2, 1, W3), f32),
            pltpu.VMEM((2, 2 * N, E), bf16), pltpu.VMEM((2, 2, N, E), bf16), pltpu.VMEM((2, 2 * N, E), bf16),
            pltpu.VMEM((2, N, E), f32),
            dma((2,)), dma((2, 4)), dma((2, 4)),
            dma((2, 2, C)), dma((2, 2, C)), dma((2, 2, C)), dma((2, 2, C)), dma((2, 2, C)),
            dma((2, 2, C)), dma((2, 2, C)), dma((2, C)),
        ],
        compiler_params=pltpu.CompilerParams(
            collective_id=0, has_side_effects=True, vmem_limit_bytes=60 * 1024 * 1024),
        cost_estimate=pl.CostEstimate(flops=11_000_000_000, bytes_accessed=8_000_000,
                                      transcendentals=11_000_000),
    )(queries, documents, positives)


def solution(mesh):
    return jax.shard_map(
        per_device,
        mesh=mesh,
        in_specs=(P(("dx", "dy"), None), P(("dx", "dy"), None), P(("dx", "dy"))),
        out_specs=(P(("dx", "dy")), P(("dx", "dy"), None), P(("dx", "dy"), None)),
        check_vma=False,
    )
```
